256 devices in a mesh: src: 16 (over z, y_lo), row: 16 (over x, y_hi, core).
Axes of the slice: x: 4, y: 4 (y_hi: 2, y_lo: 2; y = y_hi * 2 + y_lo), z: 8, core: 2. Of those that a mesh axis runs over, the one named last changes fastest.
Arguments:
- pupil: float32 [2, 1024, 1024], P(None, None, 'row'), may hold values from -6 to 6
- mask_spectrum: bfloat16 [2, 1088, 1024], P(None, None, 'row'), may hold values from -6 to 6
- shifts: int32 [32, 2], P('src'), may hold values from 0 to 63, as said below
- weights: float32 [32], P('src'), may hold values from 0.25 to 1
- measured: float32 [1024, 4096], P('row'), may hold values from 0.5 to 5
Outputs:
- pupil_grad: float32 [2, 1024, 1024], P(None, 'src', 'row')
- intensity: float32 [1024, 4096], P('row', 'src')
The draws below stay inside these ranges and needn't reach their ends.
Inputs may be any that keep to these rules, and one draw needn't show every extreme that they name: `shifts`: column 0 is a row offset, column 1 a column offset; each column takes the value 0 at some source point and 63 at some source point.
All inputs are finite; a program needn't handle non-finite values.
Results may differ from the reference program's by a relative error of at most 0.0061.
Values may be sent and summed in bfloat16 or wider, within the bound.
No kernel may reach another device: no remote copies, remote signals or barrier semaphores. Data moves between devices by JAX's collectives and lax.ppermute only.
A program may use at most 192 MiB of HBM per device.

```python
import math
import jax
import jax.numpy as jnp
from jax import lax

K = 1024
NC = 4096
NR = 1024
SOURCES = 32
SH = 64


def draw_shifts(key, part):
    key = jax.random.fold_in(key, 7)
    first_key, second_key = jax.random.split(key)
    offsets = jax.random.randint(first_key, (SOURCES, 2), 0, SH)
    chosen = jax.random.permutation(second_key, SOURCES)
    offsets = offsets.at[chosen[0], 0].set(SH - 1)
    offsets = offsets.at[chosen[0], 1].set(0)
    offsets = offsets.at[chosen[1], 0].set(0)
    offsets = offsets.at[chosen[1], 1].set(SH - 1)
    return offsets.astype(jnp.int32)


def level_of(stream_key, shape, cuts, least, top_value):
    level, own = 1.0, jax.random.fold_in(stream_key, 6)
    for axis_at, blocks in cuts:
        draws = jnp.exp(jax.random.uniform(jax.random.fold_in(own, axis_at), (blocks,), jnp.float32, least / len(cuts), top_value / len(cuts)))
        level = level * jnp.repeat(draws, shape[axis_at] // blocks).reshape([-1 if axis == axis_at else 1 for axis in range(len(shape))])
    return level


def gaussian(stream_key, dims, scale, reach, shards=(), kind=jnp.bfloat16):
    drawn = scale * jax.random.normal(stream_key, dims, jnp.float32)
    if shards:
        drawn = drawn * level_of(stream_key, dims, shards, -0.22, 0.18)
    return jnp.clip(drawn, -reach, reach).astype(kind)


def setup_inputs(seed: int = 0) -> dict:
    arg_keys = jax.random.split(jax.random.key(seed), 6)
    return {
        "pupil": gaussian(arg_keys[0], (2, K, K), 1.0, 6.0, ((2, 16),), jnp.float32),
        "mask_spectrum": gaussian(arg_keys[1], (2, K + SH, K), 1.0, 6.0, ((2, 16),)),
        "shifts": draw_shifts(jax.random.fold_in(arg_keys[5], 71), 0),
        "weights": jnp.clip(jnp.exp(math.log(1.0) - 1.3862944 * jax.random.uniform(arg_keys[3], (SOURCES,), jnp.float32) ** level_of(arg_keys[3], (SOURCES,), ((0, 16),), -0.2, 0.2)), 0.25, 1.0),
        "measured": jnp.clip(jnp.exp(math.log(5.0) - 2.3025851 * jax.random.uniform(arg_keys[4], (NR, NC), jnp.float32) ** level_of(arg_keys[4], (NR, NC), ((0, 16),), -0.2, 0.2)), 0.5, 5.0),
    }


def phase_tables(first_pos, pos_count, freq_count, period):
    positions = first_pos + lax.iota(jnp.int32, pos_count)
    frequency = lax.iota(jnp.int32, freq_count) - freq_count // 2
    turn_count = jnp.mod(positions[:, None] * frequency[None, :], period)
    phase_angle = turn_count.astype(jnp.float32) * (2.0 * math.pi / period)
    return (jnp.cos(phase_angle).astype(jnp.bfloat16), jnp.sin(phase_angle).astype(jnp.bfloat16))

def product(left_side, right_side):
    return jnp.dot(left_side, right_side, preferred_element_type=jnp.float32)

def reference(pupil, mask_spectrum, shifts, weights, measured):
    padded = jnp.pad(mask_spectrum, ((0, 0), (0, 0), (0, SH)))
    cosine_rows, sine_rows = phase_tables(0, NR, K, NC)
    cosine_cols, sine_cols = phase_tables(0, NC, K, NC)
    grad_scale = 2.0 / math.sqrt(SOURCES * NR * NC)

    def source_field(source_index):
        offsets = shifts[source_index].astype(jnp.int32)
        window = lax.dynamic_slice(padded, (jnp.int32(0), offsets[0], offsets[1]), (2, K, K)).astype(jnp.float32)
        pupil_real = (pupil[0] * window[0] - pupil[1] * window[1]).astype(jnp.bfloat16)
        pupil_imag = (pupil[0] * window[1] + pupil[1] * window[0]).astype(jnp.bfloat16)
        rows_real = ((product(cosine_rows, pupil_real) - product(sine_rows, pupil_imag)) * (1.0 / K)).astype(jnp.bfloat16)
        rows_imag = ((product(cosine_rows, pupil_imag) + product(sine_rows, pupil_real)) * (1.0 / K)).astype(jnp.bfloat16)
        field_real = product(rows_real, cosine_cols.T) - product(rows_imag, sine_cols.T)
        field_imag = product(rows_real, sine_cols.T) + product(rows_imag, cosine_cols.T)
        return (window, field_real, field_imag)

    def add_intensity(running, source_index):
        window, field_real, field_imag = source_field(source_index)
        term = weights[source_index] * (field_real * field_real + field_imag * field_imag) / SOURCES
        return (running + term, None)
    source_ids = jnp.arange(SOURCES, dtype=jnp.int32)
    intensity, _ = lax.scan(add_intensity, jnp.zeros((NR, NC), jnp.float32), source_ids)
    residual = intensity - measured

    def add_gradient(running, source_index):
        window, field_real, field_imag = source_field(source_index)
        factor = grad_scale * weights[source_index] * residual
        weighted_real = (factor * field_real).astype(jnp.bfloat16)
        weighted_imag = (factor * field_imag).astype(jnp.bfloat16)
        back_real = (product(weighted_real, cosine_cols) + product(weighted_imag, sine_cols)).astype(jnp.bfloat16)
        back_imag = (product(weighted_imag, cosine_cols) - product(weighted_real, sine_cols)).astype(jnp.bfloat16)
        spectrum_real = product(cosine_rows.T, back_real) + product(sine_rows.T, back_imag)
        spectrum_imag = product(cosine_rows.T, back_imag) - product(sine_rows.T, back_real)
        grad_real = window[0] * spectrum_real + window[1] * spectrum_imag
        grad_imag = window[0] * spectrum_imag - window[1] * spectrum_real
        return (running + jnp.stack([grad_real, grad_imag]), None)
    pupil_grad, _ = lax.scan(add_gradient, jnp.zeros((2, K, K), jnp.float32), source_ids)
    return (pupil_grad, intensity)
```

```python
import functools
import math

import jax
import jax.numpy as jnp
import ml_dtypes
import numpy as np
from jax import lax
from jax.experimental import pallas as pl
from jax.experimental.pallas import tpu as pltpu
from jax.sharding import Mesh, PartitionSpec as P

K = 1024
NC = 4096
NR = 1024
SOURCES = 32
SH = 64
NZ = 8
NYL = 2
NROW = 16
DEST = NYL * NROW
GRAD_SCALE = 2.0 / math.sqrt(SOURCES * NR * NC)
VMEM_LIMIT = 56 * 1024 * 1024
F32 = jnp.float32
BF16 = jnp.bfloat16
NT = (((1,), (1,)), ((), ()))
TN = (((0,), (0,)), ((), ()))


def phase(position, frequency):
    turns = np.mod(position * frequency, NC).astype(np.float32)
    angle = turns * np.float32(2.0 * math.pi / NC)
    return np.cos(angle), np.sin(angle)


@functools.cache
def row_tables():
    z, i, yl, row = np.meshgrid(np.arange(NZ), np.arange(4), np.arange(NYL), np.arange(NROW), indexing="ij")
    x = (64 * row + 8 * z + 4 * yl + i).reshape(NZ, 128, 1)
    cosine, sine = phase(x, np.arange(K) - K // 2)
    return np.concatenate([cosine, sine], axis=1).astype(ml_dtypes.bfloat16)


@functools.cache
def col_tables():
    f0, q, rr, k1 = np.meshgrid(np.arange(4), np.arange(4), np.arange(4), np.arange(16), indexing="ij")
    f = (64 * (4 * q + rr) + 4 * k1 + f0 - K // 2).reshape(4, 4, 64, 1)
    cosine, sine = phase(f, np.arange(1024))
    return np.stack([cosine, sine], axis=2).reshape(4, 512, 1024).astype(ml_dtypes.bfloat16)


@functools.cache
def lane_order():
    rr, c, k = np.meshgrid(np.arange(4), np.arange(2), np.arange(64), indexing="ij")
    target = (k % 4) * 128 + c * 64 + rr * 16 + k // 4
    order = np.zeros((512, 512), np.float32)
    order[np.arange(512), target.reshape(-1)] = 1.0
    return order.astype(ml_dtypes.bfloat16)


def lane_sign(shape):
    lane = lax.broadcasted_iota(jnp.int32, shape, len(shape) - 1)
    return jnp.where((lane & 127) < 64, 1.0, -1.0).astype(F32)


def rows_kernel(scal, table, here, beyond, pupil, out, windows, mask, wide, field, sums):
    mask[...] = jnp.concatenate([here[...], beyond[...]], axis=2)
    column = lax.broadcasted_iota(jnp.int32, (64, 128), 1) - lax.broadcasted_iota(jnp.int32, (64, 128), 0)
    lane = lax.broadcasted_iota(jnp.int32, (64, 128), 1)
    sign = -lane_sign((128, 128))

    def group(g, carry):
        picks = []
        for m in range(4):
            b = scal[2 * g + m // 2, 3 * (m % 2) + 1].astype(jnp.int32)
            picks.append(jnp.where(column == b, 1.0, 0.0).astype(BF16))
        pick = jnp.concatenate(picks, axis=0)
        for c in range(2):
            wide[c, :, : K + SH] = lax.dot_general(pick, mask[c], NT, preferred_element_type=F32)
        for m in range(4):
            a = scal[2 * g + m // 2, 3 * (m % 2)].astype(jnp.int32)
            rows = slice(m * 64, (m + 1) * 64)
            turn = (128 - a) & 127
            keep = lane < 128 - a
            rolled = [
                pltpu.roll(wide[c, rows, 0:128], turn, 1) for c in range(2)
            ]
            for t in range(8):
                cols = slice(t * 128, (t + 1) * 128)
                after = slice((t + 1) * 128, (t + 2) * 128)
                following = [pltpu.roll(wide[c, rows, after], turn, 1) for c in range(2)]
                wr, wi = [jnp.where(keep, rolled[c], following[c]) for c in range(2)]
                rolled = following
                pr, pi = pupil[0, :, cols], pupil[1, :, cols]
                field[m * 128 : m * 128 + 64, cols] = (pr * wr - pi * wi).astype(BF16)
                field[m * 128 + 64 : m * 128 + 128, cols] = (pr * wi + pi * wr).astype(BF16)
                windows[4 * g + m, 0:64, cols] = wr.astype(BF16)
                windows[4 * g + m, 64:128, cols] = wi.astype(BF16)
        for pair in range(2):
            both = lax.dot_general(
                table[...], field[pair * 256 : (pair + 1) * 256, :], NT, preferred_element_type=F32
            )
            for n in range(2):
                m = 2 * pair + n
                root = scal[2 * g + pair, 3 * n + 2] * (1.0 / K)
                by_cos = both[:128, n * 128 : (n + 1) * 128]
                by_sin = both[128:, n * 128 : (n + 1) * 128]
                mixed = (by_cos + sign * pltpu.roll(by_sin, 64, 1)) * root
                for i in range(4):
                    sums[pl.ds((4 * g + m) * 4 + i, 32, stride=64), :] = mixed[i * 32 : (i + 1) * 32]
        return carry

    lax.fori_loop(0, 4, group, 0)
    out[...] = sums[...].reshape(DEST, 64, 128).astype(BF16)


def image_kernel(x, order, table, measured, y, intensity, left, back, parts):
    sign = lane_sign((128, 128))
    for q in range(4):
        lined = jnp.concatenate(
            [jnp.concatenate([x[yl * 16 + 4 * q + rr] for yl in range(2)], axis=0) for rr in range(4)], axis=1
        )
        sorted_lanes = jnp.dot(lined, order[...], preferred_element_type=F32)
        for f0 in range(4):
            tile = sorted_lanes[:, f0 * 128 : (f0 + 1) * 128]
            left[f0, 0:128, q * 128 : (q + 1) * 128] = (tile * sign).astype(BF16)
            left[f0, 128:256, q * 128 : (q + 1) * 128] = pltpu.roll(tile, 64, 1).astype(BF16)

    upper = lax.broadcasted_iota(jnp.int32, (8, 128), 0) < 4
    for n in range(4):
        cols = slice(n * 256, (n + 1) * 256)
        h = [jnp.dot(left[f0], table[f0, :, cols], preferred_element_type=F32) for f0 in range(4)]
        s02, d02, s13, d13 = h[0] + h[2], h[0] - h[2], h[1] + h[3], h[1] - h[3]
        turned = jnp.concatenate([-d13[128:], d13[:128]], axis=0)
        fields = [s02 + s13, d02 + turned, s02 - s13, d02 - turned]
        scaled = []
        for y1 in range(4):
            e = fields[y1].reshape(2, 16, 8, 256)
            power = jnp.sum(e[0] * e[0] + e[1] * e[1], axis=0)
            power = (power + pltpu.roll(power, 4, 0)) * (1.0 / SOURCES)
            intensity[y1 * 4 + n] = jnp.where(upper, power[:, :128], power[:, 128:])
            residual = power - measured[:, y1 * 1024 + n * 256 : y1 * 1024 + (n + 1) * 256]
            scaled.append((e * (residual * GRAD_SCALE)[None, None]).reshape(256, 256))
        s02, d02 = scaled[0] + scaled[2], scaled[0] - scaled[2]
        s13, d13 = scaled[1] + scaled[3], scaled[1] - scaled[3]
        turned = jnp.concatenate([-d13[128:], d13[:128]], axis=0)
        back[0, :, cols] = (s02 + s13).astype(BF16)
        back[1, :, cols] = (d02 - turned).astype(BF16)
        back[2, :, cols] = (s02 - s13).astype(BF16)
        back[3, :, cols] = (d02 + turned).astype(BF16)

    for f0 in range(4):
        both = lax.dot_general(back[f0], table[f0], NT, preferred_element_type=F32)
        for q in range(4):
            cols = slice(q * 128, (q + 1) * 128)
            mixed = sign * both[:128, cols] + pltpu.roll(both[128:, cols], 64, 1)
            parts[q, :, f0 * 128 : (f0 + 1) * 128] = mixed.astype(BF16)
    for q in range(4):
        lined = lax.dot_general(parts[q], order[...], NT, preferred_element_type=F32).astype(BF16)
        for rr in range(4):
            for yl in range(2):
                y[yl * 16 + 4 * q + rr] = lined[yl * 64 : (yl + 1) * 64, rr * 128 : (rr + 1) * 128]


def gradient_kernel(scal, y, table, windows, intensity, out, rows, total):
    rows[...] = y[...].astype(F32).reshape(DEST * 64, 128)
    sign = lane_sign((128, 128))
    total[...] = jnp.zeros_like(total)

    def group(g, carry):
        lefts = []
        for m in range(4):
            u = jnp.concatenate(
                [rows[pl.ds((4 * g + m) * 4 + i, 32, stride=64), :] for i in range(4)], axis=0
            )
            lefts.append(jnp.concatenate([u, sign * pltpu.roll(u, 64, 1)], axis=0).astype(BF16))
        left = jnp.concatenate(lefts, axis=1)
        for n in range(4):
            cols = slice(n * 256, (n + 1) * 256)
            v = lax.dot_general(left, table[:, cols], TN, preferred_element_type=F32)
            real, imag = total[0:64, cols], total[64:128, cols]
            for m in range(4):
                root = scal[2 * g + m // 2, 3 * (m % 2) + 2]
                vr, vi = v[m * 128 : m * 128 + 64], v[m * 128 + 64 : m * 128 + 128]
                w = windows[4 * g + m, :, cols].astype(F32) * root
                wr, wi = w[:64], w[64:]
                real = real + wr * vr + wi * vi
                imag = imag + wr * vi - wi * vr
            total[0:64, cols] = real
            total[64:128, cols] = imag
        return carry

    lax.fori_loop(0, 4, group, 0)
    for t in range(8):
        turned = total[:, t * 128 : (t + 1) * 128].T.astype(BF16)
        for n in range(2):
            out[2 * t + n, 0:64] = turned[n * 64 : (n + 1) * 64]
    power = intensity[...]
    coarse = power.astype(BF16)
    fine = power - coarse.astype(F32)
    out[:, 64:80] = jnp.concatenate([coarse.astype(F32), fine], axis=1).astype(BF16)


def vmem(count):
    return [pl.BlockSpec(memory_space=pltpu.VMEM)] * count


SMEM = pl.BlockSpec(memory_space=pltpu.SMEM)
PARAMS = pltpu.CompilerParams(vmem_limit_bytes=VMEM_LIMIT)


def rows_call(scal, table, here, beyond, pupil):
    return pl.pallas_call(
        rows_kernel,
        out_shape=(
            jax.ShapeDtypeStruct((DEST, 64, 128), BF16),
            jax.ShapeDtypeStruct((16, 128, K), BF16),
        ),
        in_specs=[SMEM] + vmem(4),
        out_specs=tuple(vmem(2)),
        scratch_shapes=[
            pltpu.VMEM((2, K + SH, 128), BF16),
            pltpu.VMEM((2, 256, K + 128), F32),
            pltpu.VMEM((512, K), BF16),
            pltpu.VMEM((DEST * 64, 128), F32),
        ],
        compiler_params=PARAMS,
        name="rows",
    )(scal, table, here, beyond, pupil)


def image_call(x, measured):
    return pl.pallas_call(
        image_kernel,
        out_shape=(
            jax.ShapeDtypeStruct((DEST, 64, 128), BF16),
            jax.ShapeDtypeStruct((16, 8, 128), F32),
        ),
        in_specs=vmem(4),
        out_specs=tuple(vmem(2)),
        scratch_shapes=[
            pltpu.VMEM((4, 256, 512), BF16),
            pltpu.VMEM((4, 256, 1024), BF16),
            pltpu.VMEM((4, 128, 512), BF16),
        ],
        compiler_params=PARAMS,
        name="image",
    )(x, jnp.asarray(lane_order()), jnp.asarray(col_tables()), measured)


def gradient_call(scal, y, table, windows, intensity):
    return pl.pallas_call(
        gradient_kernel,
        out_shape=jax.ShapeDtypeStruct((16, 80, 128), BF16),
        in_specs=[SMEM] + vmem(4),
        out_specs=vmem(1)[0],
        scratch_shapes=[
            pltpu.VMEM((DEST * 64, 128), F32),
            pltpu.VMEM((128, K), F32),
        ],
        compiler_params=PARAMS,
        name="gradient",
    )(scal, y, table, windows, intensity)


def exchange(blocks, axes):
    return lax.all_to_all(blocks, axes, split_axis=0, concat_axis=0, tiled=True)


def shards(pupil, mask_spectrum, shifts, weights, measured):
    z, yl = lax.axis_index("z"), lax.axis_index("yl")
    own = jnp.concatenate([shifts.astype(F32), jnp.sqrt(weights)[:, None]], axis=1).reshape(1, 6)
    scal = exchange(jnp.tile(own, (NZ, 1)), "z")
    beyond = lax.ppermute(mask_spectrum, "row", [(i + 1, i) for i in range(NROW - 1)])
    table = lax.dynamic_index_in_dim(jnp.asarray(row_tables()), z, 0, keepdims=False)
    four = lax.dynamic_slice(measured, (8 * z + 4 * yl, 0), (4, NC))
    four = jnp.concatenate([four, four], axis=0)
    blocks, windows = rows_call(scal, table, mask_spectrum, beyond, pupil.transpose(0, 2, 1))
    blocks, intensity = image_call(exchange(blocks, ("yl", "row")), four)
    blocks = exchange(blocks, ("yl", "row"))
    parts = exchange(gradient_call(scal, blocks, table, windows, intensity), ("z", "yl"))
    grad = jnp.sum(parts[:, :64].astype(F32), axis=0).reshape(64, 2, 64).transpose(1, 0, 2)
    image = (parts[:, 64:72].astype(F32) + parts[:, 72:80].astype(F32)).reshape(16, 2, 4, 128)
    return grad, image.transpose(0, 2, 1, 3).reshape(64, 256)


def solution(mesh):
    finer = Mesh(mesh.devices.reshape(NZ, NYL, NROW), ("z", "yl", "row"))
    src = ("z", "yl")
    return jax.shard_map(
        shards,
        mesh=finer,
        in_specs=(
            P(None, None, "row"),
            P(None, None, "row"),
            P(src, None),
            P(src),
            P("row", None),
        ),
        out_specs=(P(None, src, "row"), P("row", src)),
        check_vma=False,
    )
```

```python
import functools
import math

import jax
import jax.numpy as jnp
import ml_dtypes
import numpy as np
from jax import lax
from jax.experimental import pallas as pl
from jax.experimental.pallas import tpu as pltpu
from jax.sharding import Mesh, PartitionSpec as P

K = 1024
NC = 4096
NR = 1024
SOURCES = 32
SH = 64
NZ = 8
NYL = 2
NROW = 16
DEST = NYL * NROW
GRAD_SCALE = 2.0 / math.sqrt(SOURCES * NR * NC)
VMEM_LIMIT = 20 * 1024 * 1024
F32 = jnp.float32
BF16 = jnp.bfloat16
NT = (((1,), (1,)), ((), ()))
TN = (((0,), (0,)), ((), ()))


def phase(position, frequency):
    turns = np.mod(position * frequency, NC).astype(np.float32)
    angle = turns * np.float32(2.0 * math.pi / NC)
    return np.cos(angle), np.sin(angle)


@functools.cache
def row_tables():
    z, yl, row, i = np.meshgrid(np.arange(NZ), np.arange(NYL), np.arange(NROW), np.arange(4), indexing="ij")
    x = (64 * row + 8 * z + 4 * yl + i).reshape(NZ, 128, 1)
    cosine, sine = phase(x, np.arange(K) - K // 2)
    return np.concatenate([cosine, sine], axis=1).astype(ml_dtypes.bfloat16)


@functools.cache
def col_tables():
    f0, q, rr, k1 = np.meshgrid(np.arange(4), np.arange(4), np.arange(4), np.arange(16), indexing="ij")
    f = (64 * (4 * q + rr) + 4 * k1 + f0 - K // 2).reshape(4, 4, 64, 1)
    cosine, sine = phase(f, np.arange(1024))
    return np.stack([cosine, sine], axis=2).reshape(4, 512, 1024).astype(ml_dtypes.bfloat16)


@functools.cache
def lane_order():
    rr, c, k = np.meshgrid(np.arange(4), np.arange(2), np.arange(64), indexing="ij")
    target = (k % 4) * 128 + c * 64 + rr * 16 + k // 4
    order = np.zeros((512, 512), np.float32)
    order[np.arange(512), target.reshape(-1)] = 1.0
    return order.astype(ml_dtypes.bfloat16)


def lane_sign(shape):
    lane = lax.broadcasted_iota(jnp.int32, shape, len(shape) - 1)
    return jnp.where((lane & 127) < 64, 1.0, -1.0).astype(F32)


def root_columns(low, high):
    lane = lax.broadcasted_iota(jnp.int32, (128, 128), 1)
    return jnp.where((lane & 32) == 0, low, high)


def swap_rows(a, b):
    low = lax.broadcasted_iota(jnp.int32, a.shape, 1) < 4
    return jnp.where(low, a, pltpu.roll(b, 4, 1)), jnp.where(low, pltpu.roll(a, 4, 1), b)


def stage_kernel(place, here, pupil, measured, mask, share, four, eight, arrived):
    rows = pl.ds(pl.multiple_of(place[0] * 8, 8), 8)
    copy = pltpu.make_async_copy(measured.at[rows, :], eight, arrived)
    copy.start()
    first = pl.multiple_of(place[1] * 32, 32)
    for c in range(2):
        for t in range(9):
            width = 128 if t < 8 else SH
            mask[c, t, :, :width] = here[c, :, t * 128 : t * 128 + width].astype(F32)
        for t in range(8):
            share[c, t] = pupil[c, pl.ds(first, 32), t * 128 : (t + 1) * 128]
    copy.wait()
    upper = lax.broadcasted_iota(jnp.int32, (8, NC), 0) >= 4
    wanted = upper == (place[1] == 1)
    four[...] = jnp.where(wanted, eight[...], pltpu.roll(eight[...], 4, 0))


def rows_kernel(
    gathered, table, here, beyond, share, far, out, windows, roots, near, scal, mask, fields, arrived, loaded
):
    copy = pltpu.make_async_copy(gathered, scal, arrived)
    copy.start()
    load = pltpu.make_async_copy(far, near, loaded)
    load.start()
    for c in range(2):
        for t in range(9):
            width = 128 if t < 8 else SH
            mask[c, t, 0:64, :width] = here[c, t, :, :width]
            mask[c, t, 64:128, :width] = beyond[c, :, t * 128 : t * 128 + width].astype(F32)
    copy.wait()
    for m in range(2):
        for p in range(16):
            at = m * 64 + p * 4
            roots[at : at + 4, :] = jnp.full((4, 128), scal[p, 0, 3 * m + 2])
    lane = lax.broadcasted_iota(jnp.int32, (32, 128), 1)
    sign = -lane_sign((128, 128))

    def build(p, field, at):
        first = [scal[p, 0, 3 * m + 1].astype(jnp.int32) for m in range(2)]
        by = [scal[p, 0, 3 * m].astype(jnp.int32) for m in range(2)]
        turn = [(128 - a) & 127 for a in by]
        keep = [lane < 128 - a for a in by]

        def turned(c, t, m):
            return pltpu.roll(mask[c, t, pl.ds(first[m], 32), :], turn[m], 1)

        before = [[turned(c, 0, m) for c in range(2)] for m in range(2)]
        for t in range(8):
            cols = slice(t * 128, (t + 1) * 128)
            pr, pi = share[0, t], share[1, t]
            for m in range(2):
                after = [turned(c, t + 1, m) for c in range(2)]
                wr, wi = [jnp.where(keep[m], before[m][c], after[c]) for c in range(2)]
                before[m] = after
                low, high = m * 32, 64 + m * 32
                field[at + low : at + low + 32, cols] = (pr * wr - pi * wi).astype(BF16)
                field[at + high : at + high + 32, cols] = (pr * wi + pi * wr).astype(BF16)
                windows[p, low : low + 32, cols] = wr.astype(BF16)
                windows[p, high : high + 32, cols] = wi.astype(BF16)

    def transform(g, field):
        mixed = []
        for half in range(2):
            rows = field[half * 256 : (half + 1) * 256, :]
            both = lax.dot_general(table[...], rows, NT, preferred_element_type=F32)
            for n in range(2):
                p = 4 * g + 2 * half + n
                by_cos = both[:128, n * 128 : (n + 1) * 128]
                by_sin = both[128:, n * 128 : (n + 1) * 128]
                root = root_columns(scal[p, 0, 2], scal[p, 0, 5]) * (1.0 / K)
                mixed.append(((by_cos + sign * pltpu.roll(by_sin, 64, 1)) * root).reshape(16, 8, 128))
        first, second = swap_rows(mixed[0], mixed[1]), swap_rows(mixed[2], mixed[3])
        for n in range(2):
            tile = jnp.concatenate([first[n], second[n]], axis=1).astype(BF16)
            out[:, n, g * 16 : (g + 1) * 16, :] = tile

    for g in range(5):
        if g < 4:
            for n in range(4):
                build(4 * g + n, fields.at[g], n * 128)
        if g > 0:
            transform(g - 1, fields.at[g - 1])
    load.wait()


def swap_halves(a, b):
    low = (lax.broadcasted_iota(jnp.int32, a.shape, 1) & 32) == 0
    return jnp.where(low, a, pltpu.roll(b, 32, 1)), jnp.where(low, pltpu.roll(a, 96, 1), b)


def image_kernel(x, order, table, measured, roots, y, intensity, left, back, parts):
    sign = lane_sign((128, 128))
    for q in range(4):
        tiles = []
        for rr in range(4):
            r = 4 * q + rr
            tiles.append(jnp.concatenate(swap_halves(x[r].astype(F32), x[16 + r].astype(F32)), axis=0))
        lined = jnp.concatenate(tiles, axis=1).astype(BF16)
        sorted_lanes = jnp.dot(lined, order[...], preferred_element_type=F32)
        for f0 in range(4):
            tile = sorted_lanes[:, f0 * 128 : (f0 + 1) * 128]
            left[f0, 0:128, q * 128 : (q + 1) * 128] = (tile * sign).astype(BF16)
            left[f0, 128:256, q * 128 : (q + 1) * 128] = pltpu.roll(tile, 64, 1).astype(BF16)

    upper = lax.broadcasted_iota(jnp.int32, (8, 128), 0) < 4
    for n in range(4):
        cols = slice(n * 256, (n + 1) * 256)
        h = [jnp.dot(left[f0], table[f0, :, cols], preferred_element_type=F32) for f0 in range(4)]
        s02, d02, s13, d13 = h[0] + h[2], h[0] - h[2], h[1] + h[3], h[1] - h[3]
        turned = jnp.concatenate([-d13[128:], d13[:128]], axis=0)
        fields = [s02 + s13, d02 + turned, s02 - s13, d02 - turned]
        scaled = []
        for y1 in range(4):
            e = fields[y1].reshape(2, 16, 8, 256)
            power = jnp.sum(e[0] * e[0] + e[1] * e[1], axis=0)
            power = (power + pltpu.roll(power, 4, 0)) * (1.0 / SOURCES)
            intensity[y1 * 4 + n] = jnp.where(upper, power[:, :128], power[:, 128:])
            residual = power - measured[:, y1 * 1024 + n * 256 : y1 * 1024 + (n + 1) * 256]
            scaled.append((e * (residual * GRAD_SCALE)[None, None]).reshape(256, 256))
        s02, d02 = scaled[0] + scaled[2], scaled[0] - scaled[2]
        s13, d13 = scaled[1] + scaled[3], scaled[1] - scaled[3]
        turned = jnp.concatenate([-d13[128:], d13[:128]], axis=0)
        back[0, :, cols] = (s02 + s13).astype(BF16)
        back[1, :, cols] = (d02 - turned).astype(BF16)
        back[2, :, cols] = (s02 - s13).astype(BF16)
        back[3, :, cols] = (d02 + turned).astype(BF16)

    for f0 in range(4):
        both = lax.dot_general(back[f0], table[f0], NT, preferred_element_type=F32)
        for q in range(4):
            cols = slice(q * 128, (q + 1) * 128)
            mixed = sign * both[:128, cols] + pltpu.roll(both[128:, cols], 64, 1)
            parts[q, :, f0 * 128 : (f0 + 1) * 128] = (mixed * roots[...]).astype(BF16)
    for q in range(4):
        lined = lax.dot_general(parts[q], order[...], NT, preferred_element_type=F32)
        for rr in range(4):
            tile = lined[:, rr * 128 : (rr + 1) * 128]
            low, high = swap_halves(tile[:64], tile[64:])
            y[4 * q + rr] = low.astype(BF16)
            y[16 + 4 * q + rr] = high.astype(BF16)


def gradient_kernel(y, table, windows, intensity, out, total):
    sign = lane_sign((128, 128))
    total[...] = jnp.zeros_like(total)

    def group(g, carry):
        tiles = [y[:, n, pl.ds(pl.multiple_of(g * 16, 16), 16), :].astype(F32) for n in range(2)]
        lefts = []
        for half in range(2):
            part = slice(half * 8, (half + 1) * 8)
            for u in swap_rows(tiles[0][:, part], tiles[1][:, part]):
                u = u.reshape(128, 128)
                lefts.append(jnp.concatenate([u, sign * pltpu.roll(u, 64, 1)], axis=0).astype(BF16))
        left = jnp.concatenate(lefts, axis=1)
        for n in range(4):
            cols = slice(n * 256, (n + 1) * 256)
            v = lax.dot_general(left, table[:, cols], TN, preferred_element_type=F32)
            real, imag = total[0:64, cols], total[64:128, cols]
            for m in range(4):
                vr, vi = v[m * 128 : m * 128 + 64], v[m * 128 + 64 : m * 128 + 128]
                w = windows[4 * g + m, :, cols].astype(F32)
                wr, wi = w[:64], w[64:]
                real = real + wr * vr + wi * vi
                imag = imag + wr * vi - wi * vr
            total[0:64, cols] = real
            total[64:128, cols] = imag
        return carry

    lax.fori_loop(0, 4, group, 0)
    for t in range(8):
        cols = slice(t * 128, (t + 1) * 128)
        real = total[0:32, cols] + total[32:64, cols]
        imag = total[64:96, cols] + total[96:128, cols]
        turned = jnp.concatenate([real, imag], axis=0).T
        for n in range(2):
            both = jnp.concatenate([turned[n * 64 : n * 64 + 32], turned[n * 64 + 32 : n * 64 + 64]], axis=1)
            out[2 * t + n, 0:32] = both.astype(BF16)
    power = intensity[...]
    coarse = power.astype(BF16).astype(F32)
    out[:, 32:48] = jnp.concatenate([coarse, power - coarse], axis=1).astype(BF16)


def final_kernel(parts, grad, image):
    for yl in range(2):
        total = jnp.sum(
            jnp.stack([parts[2 * z + yl, 0:32].astype(F32) for z in range(NZ)]), axis=0
        )
        for h in range(2):
            for c in range(2):
                start = h * 64 + c * 32
                grad[c, h * 32 : (h + 1) * 32, yl * 32 : (yl + 1) * 32] = total[:, start : start + 32]
    for j in range(16):
        both = parts[j, 32:48].astype(F32)
        power = both[:8] + both[8:]
        for h in range(2):
            image[4 * j : 4 * j + 4, h * 128 : (h + 1) * 128] = power[4 * h : 4 * h + 4]


def vmem(count):
    return [pl.BlockSpec(memory_space=pltpu.VMEM)] * count


HBM = pl.BlockSpec(memory_space=pltpu.HBM)
ANY = pl.BlockSpec(memory_space=pl.ANY)
SMEM = pl.BlockSpec(memory_space=pltpu.SMEM)
SMALL = pltpu.CompilerParams(vmem_limit_bytes=6 * 1024 * 1024)
PARAMS = pltpu.CompilerParams(vmem_limit_bytes=VMEM_LIMIT)


def kept(array):
    return pltpu.with_memory_space_constraint(array, pltpu.VMEM)


def own_kernel(shifts, weights, out):
    place = lax.broadcasted_iota(jnp.int32, (16, 128), 1)
    column = ((lax.broadcasted_iota(jnp.int32, (16, 128), 0) & 1) * 32).astype(F32)
    own = column
    for m in range(2):
        own = jnp.where(place == 3 * m, shifts[m, 0].astype(F32), own)
        own = jnp.where(place == 3 * m + 1, shifts[m, 1].astype(F32) + column, own)
        own = jnp.where(place == 3 * m + 2, jnp.sqrt(jnp.full((16, 128), weights[m])), own)
    out[:, 0, :] = own


def own_call(shifts, weights):
    return pl.pallas_call(
        own_kernel,
        out_shape=jax.ShapeDtypeStruct((16, 1, 128), F32),
        in_specs=[SMEM, SMEM],
        out_specs=vmem(1)[0],
        name="own",
    )(shifts, weights)


def stage_call(place, here, pupil, measured):
    return pl.pallas_call(
        stage_kernel,
        out_shape=(
            pltpu.VMEM((2, 9, 64, 128), F32),
            pltpu.VMEM((2, 8, 32, 128), F32),
            pltpu.VMEM((8, NC), F32),
        ),
        in_specs=[SMEM] + vmem(2) + [HBM],
        out_specs=tuple(vmem(3)),
        scratch_shapes=[pltpu.VMEM((8, NC), F32), pltpu.SemaphoreType.DMA],
        compiler_params=SMALL,
        name="stage",
    )(place, here, pupil, pltpu.with_memory_space_constraint(measured, pltpu.HBM))


def rows_call(scal, table, here, beyond, share):
    far = pltpu.with_memory_space_constraint(jnp.asarray(col_tables()), pltpu.HBM)
    return pl.pallas_call(
        rows_kernel,
        out_shape=(
            jax.ShapeDtypeStruct((16, 2, 64, 128), BF16),
            pltpu.VMEM((16, 128, K), BF16),
            pltpu.VMEM((128, 128), F32),
            pltpu.VMEM((4, 512, 1024), BF16),
        ),
        in_specs=[ANY] + vmem(4) + [HBM],
        out_specs=tuple(vmem(4)),
        scratch_shapes=[
            pltpu.SMEM((16, 1, 128), F32),
            pltpu.VMEM((2, 9, 128, 128), F32),
            pltpu.VMEM((4, 512, K), BF16),
            pltpu.SemaphoreType.DMA,
            pltpu.SemaphoreType.DMA,
        ],
        compiler_params=PARAMS,
        name="rows",
    )(scal, kept(table), kept(here), kept(beyond), kept(share), far)


def image_call(x, table, measured, roots):
    return pl.pallas_call(
        image_kernel,
        out_shape=(
            jax.ShapeDtypeStruct((DEST, 64, 128), BF16),
            pltpu.VMEM((16, 8, 128), F32),
        ),
        in_specs=vmem(5),
        out_specs=tuple(vmem(2)),
        scratch_shapes=[
            pltpu.VMEM((4, 256, 512), BF16),
            pltpu.VMEM((4, 256, 1024), BF16),
            pltpu.VMEM((4, 128, 512), BF16),
        ],
        compiler_params=PARAMS,
        name="image",
    )(x, kept(jnp.asarray(lane_order())), kept(table), kept(measured), kept(roots))


def gradient_call(y, table, windows, intensity):
    return pl.pallas_call(
        gradient_kernel,
        out_shape=jax.ShapeDtypeStruct((16, 48, 128), BF16),
        in_specs=vmem(4),
        out_specs=vmem(1)[0],
        scratch_shapes=[pltpu.VMEM((128, K), F32)],
        compiler_params=PARAMS,
        name="gradient",
    )(y.reshape(16, 2, 64, 128), kept(table), kept(windows), kept(intensity))


def final_call(parts):
    return pl.pallas_call(
        final_kernel,
        out_shape=(jax.ShapeDtypeStruct((2, 64, 64), F32), jax.ShapeDtypeStruct((64, 256), F32)),
        in_specs=vmem(1),
        out_specs=tuple(vmem(2)),
        compiler_params=SMALL,
        name="final",
    )(kept(parts))


def exchange(blocks, axes):
    return lax.all_to_all(blocks, axes, split_axis=0, concat_axis=0, tiled=True)


def shards(pupil, mask_spectrum, shifts, weights, measured):
    z, yl = lax.axis_index("z"), lax.axis_index("yl")
    mask = mask_spectrum.transpose(0, 2, 1)
    own, late = lax.optimization_barrier((own_call(shifts, weights), mask))
    scal = exchange(own, ("z", "yl"))
    beyond = lax.ppermute(late, "row", [(i + 1, i) for i in range(NROW - 1)])
    place = jnp.stack([z, yl]).astype(jnp.int32)
    here, share, four = stage_call(place, mask, pupil.transpose(0, 2, 1), measured)
    table = lax.dynamic_index_in_dim(jnp.asarray(row_tables()), z, 0, keepdims=False)
    blocks, windows, roots, near = rows_call(scal, table, here, beyond, share)
    blocks, intensity = image_call(exchange(blocks.reshape(DEST, 64, 128), ("yl", "row")), near, four, roots)
    blocks = exchange(blocks, ("yl", "row"))
    parts = exchange(gradient_call(blocks, table, windows, intensity), ("z", "yl"))
    return final_call(parts)


def solution(mesh):
    finer = Mesh(mesh.devices.reshape(NZ, NYL, NROW), ("z", "yl", "row"))
    src = ("z", "yl")
    return jax.shard_map(
        shards,
        mesh=finer,
        in_specs=(
            P(None, None, "row"),
            P(None, None, "row"),
            P(src, None),
            P(src),
            P("row", None),
        ),
        out_specs=(P(None, src, "row"), P("row", src)),
        check_vma=False,
    )
```

```python
import functools
import math

import jax
import jax.numpy as jnp
import ml_dtypes
import numpy as np
from jax import lax
from jax.experimental import pallas as pl
from jax.experimental.pallas import tpu as pltpu
from jax.sharding import Mesh, PartitionSpec as P

K = 1024
NC = 4096
NR = 1024
SOURCES = 32
SH = 64
NZ = 8
NYL = 2
NROW = 16
DEST = NYL * NROW
GRAD_SCALE = 2.0 / math.sqrt(SOURCES * NR * NC)
VMEM_LIMIT = 20 * 1024 * 1024
F32 = jnp.float32
BF16 = jnp.bfloat16
NT = (((1,), (1,)), ((), ()))
TN = (((0,), (0,)), ((), ()))


def phase(position, frequency):
    turns = np.mod(position * frequency, NC).astype(np.float32)
    angle = turns * np.float32(2.0 * math.pi / NC)
    return np.cos(angle), np.sin(angle)


@functools.cache
def row_tables():
    z, yl, row, i = np.meshgrid(np.arange(NZ), np.arange(NYL), np.arange(NROW), np.arange(4), indexing="ij")
    x = (64 * row + 8 * z + 4 * yl + i).reshape(NZ, 128, 1)
    cosine, sine = phase(x, np.arange(K) - K // 2)
    return np.concatenate([cosine, sine], axis=1).astype(ml_dtypes.bfloat16)


@functools.cache
def col_tables():
    f0, q, rr, k1 = np.meshgrid(np.arange(4), np.arange(4), np.arange(4), np.arange(16), indexing="ij")
    f = (64 * (4 * q + rr) + 4 * k1 + f0 - K // 2).reshape(4, 4, 64, 1)
    cosine, sine = phase(f, np.arange(1024))
    return np.stack([cosine, sine], axis=2).reshape(4, 512, 1024).astype(ml_dtypes.bfloat16)


@functools.cache
def lane_order():
    rr, c, k = np.meshgrid(np.arange(4), np.arange(2), np.arange(64), indexing="ij")
    target = (k % 4) * 128 + c * 64 + rr * 16 + k // 4
    order = np.zeros((512, 512), np.float32)
    order[np.arange(512), target.reshape(-1)] = 1.0
    return order.astype(ml_dtypes.bfloat16)


def lane_sign(shape):
    lane = lax.broadcasted_iota(jnp.int32, shape, len(shape) - 1)
    return jnp.where((lane & 127) < 64, 1.0, -1.0).astype(F32)


def root_columns(low, high):
    lane = lax.broadcasted_iota(jnp.int32, (128, 128), 1)
    return jnp.where((lane & 32) == 0, low, high)


def swap_rows(a, b):
    low = lax.broadcasted_iota(jnp.int32, a.shape, 1) < 4
    return jnp.where(low, a, pltpu.roll(b, 4, 1)), jnp.where(low, pltpu.roll(a, 4, 1), b)


def stage_kernel(place, here, pupil, measured, mask, share, four, eight, arrived):
    rows = pl.ds(pl.multiple_of(place[0] * 8, 8), 8)
    copy = pltpu.make_async_copy(measured.at[rows, :], eight, arrived)
    copy.start()
    first = pl.multiple_of(place[1] * 32, 32)
    for c in range(2):
        for t in range(9):
            width = 128 if t < 8 else SH
            mask[c, t, :, :width] = here[c, :, t * 128 : t * 128 + width].astype(F32)
        for t in range(8):
            share[c, t] = pupil[c, pl.ds(first, 32), t * 128 : (t + 1) * 128]
    copy.wait()
    upper = lax.broadcasted_iota(jnp.int32, (8, NC), 0) >= 4
    wanted = upper == (place[1] == 1)
    four[...] = jnp.where(wanted, eight[...], pltpu.roll(eight[...], 4, 0))


def rows_kernel(
    gathered, table, here, beyond, share, far, out, windows, roots, near, scal, mask, fields, arrived, loaded
):
    copy = pltpu.make_async_copy(gathered, scal, arrived)
    copy.start()
    load = pltpu.make_async_copy(far, near, loaded)
    load.start()
    for c in range(2):
        for t in range(9):
            width = 128 if t < 8 else SH
            mask[c, t, 0:64, :width] = here[c, t, :, :width]
            mask[c, t, 64:128, :width] = beyond[c, :, t * 128 : t * 128 + width].astype(F32)
    copy.wait()
    for m in range(2):
        for p in range(16):
            at = m * 64 + p * 4
            roots[at : at + 4, :] = jnp.full((4, 128), scal[p, 0, 3 * m + 2])
    lane = lax.broadcasted_iota(jnp.int32, (32, 128), 1)
    sign = -lane_sign((128, 128))

    def build(p, field, at):
        first = [scal[p, 0, 3 * m + 1].astype(jnp.int32) for m in range(2)]
        by = [scal[p, 0, 3 * m].astype(jnp.int32) for m in range(2)]
        turn = [(128 - a) & 127 for a in by]
        keep = [lane < 128 - a for a in by]

        def turned(c, t, m):
            return pltpu.roll(mask[c, t, pl.ds(first[m], 32), :].astype(BF16), turn[m], 1)

        before = [[turned(c, 0, m) for c in range(2)] for m in range(2)]
        for t in range(8):
            cols = slice(t * 128, (t + 1) * 128)
            pr, pi = share[0, t], share[1, t]
            for m in range(2):
                after = [turned(c, t + 1, m) for c in range(2)]
                parts = [jnp.where(keep[m], before[m][c], after[c]) for c in range(2)]
                wr, wi = [part.astype(F32) for part in parts]
                before[m] = after
                low, high = m * 32, 64 + m * 32
                field[at + low : at + low + 32, cols] = (pr * wr - pi * wi).astype(BF16)
                field[at + high : at + high + 32, cols] = (pr * wi + pi * wr).astype(BF16)
                windows[p, low : low + 32, cols] = parts[0]
                windows[p, high : high + 32, cols] = parts[1]

    def transform(g, field):
        mixed = []
        for half in range(2):
            rows = field[half * 256 : (half + 1) * 256, :]
            both = lax.dot_general(table[...], rows, NT, preferred_element_type=F32)
            for n in range(2):
                p = 4 * g + 2 * half + n
                by_cos = both[:128, n * 128 : (n + 1) * 128]
                by_sin = both[128:, n * 128 : (n + 1) * 128]
                root = root_columns(scal[p, 0, 2], scal[p, 0, 5]) * (1.0 / K)
                mixed.append(((by_cos + sign * pltpu.roll(by_sin, 64, 1)) * root).reshape(16, 8, 128))
        first, second = swap_rows(mixed[0], mixed[1]), swap_rows(mixed[2], mixed[3])
        for n in range(2):
            tile = jnp.concatenate([first[n], second[n]], axis=1).astype(BF16)
            out[:, n, g * 16 : (g + 1) * 16, :] = tile

    for g in range(5):
        if g < 4:
            for n in range(4):
                build(4 * g + n, fields.at[g], n * 128)
        if g > 0:
            transform(g - 1, fields.at[g - 1])
    load.wait()


def swap_halves(a, b):
    low = (lax.broadcasted_iota(jnp.int32, a.shape, 1) & 32) == 0
    return jnp.where(low, a, pltpu.roll(b, 32, 1)), jnp.where(low, pltpu.roll(a, 96, 1), b)


def image_kernel(x, order, table, measured, roots, y, intensity, left, back, parts):
    sign = lane_sign((128, 128))
    stacked = []
    for q in range(4):
        tiles = []
        for rr in range(4):
            r = 4 * q + rr
            tiles.append(jnp.concatenate(swap_halves(x[r].astype(F32), x[16 + r].astype(F32)), axis=0))
        stacked.append(jnp.concatenate(tiles, axis=1).astype(BF16))
    sorted_lanes = jnp.dot(jnp.concatenate(stacked, axis=0), order[...], preferred_element_type=F32)
    for q in range(4):
        for f0 in range(4):
            tile = sorted_lanes[q * 128 : (q + 1) * 128, f0 * 128 : (f0 + 1) * 128]
            left[f0, 0:128, q * 128 : (q + 1) * 128] = (tile * sign).astype(BF16)
            left[f0, 128:256, q * 128 : (q + 1) * 128] = pltpu.roll(tile, 64, 1).astype(BF16)

    upper = lax.broadcasted_iota(jnp.int32, (8, 128), 0) < 4
    for n in range(4):
        cols = slice(n * 256, (n + 1) * 256)
        h = [jnp.dot(left[f0], table[f0, :, cols], preferred_element_type=F32) for f0 in range(4)]
        s02, d02, s13, d13 = h[0] + h[2], h[0] - h[2], h[1] + h[3], h[1] - h[3]
        turned = jnp.concatenate([-d13[128:], d13[:128]], axis=0)
        fields = [s02 + s13, d02 + turned, s02 - s13, d02 - turned]
        scaled = []
        for y1 in range(4):
            e = fields[y1].reshape(2, 16, 8, 256)
            power = jnp.sum(e[0] * e[0] + e[1] * e[1], axis=0)
            power = (power + pltpu.roll(power, 4, 0)) * (1.0 / SOURCES)
            intensity[y1 * 4 + n] = jnp.where(upper, power[:, :128], power[:, 128:])
            residual = power - measured[:, y1 * 1024 + n * 256 : y1 * 1024 + (n + 1) * 256]
            scaled.append((e * (residual * GRAD_SCALE)[None, None]).reshape(256, 256))
        s02, d02 = scaled[0] + scaled[2], scaled[0] - scaled[2]
        s13, d13 = scaled[1] + scaled[3], scaled[1] - scaled[3]
        turned = jnp.concatenate([-d13[128:], d13[:128]], axis=0)
        back[0, :, cols] = (s02 + s13).astype(BF16)
        back[1, :, cols] = (d02 - turned).astype(BF16)
        back[2, :, cols] = (s02 - s13).astype(BF16)
        back[3, :, cols] = (d02 + turned).astype(BF16)

    for f0 in range(4):
        both = lax.dot_general(back[f0], table[f0], NT, preferred_element_type=F32)
        for q in range(4):
            cols = slice(q * 128, (q + 1) * 128)
            mixed = sign * both[:128, cols] + pltpu.roll(both[128:, cols], 64, 1)
            parts[q, :, f0 * 128 : (f0 + 1) * 128] = (mixed * roots[...]).astype(BF16)
    lined = lax.dot_general(parts[...].reshape(512, 512), order[...], NT, preferred_element_type=F32)
    for q in range(4):
        for rr in range(4):
            tile = lined[q * 128 : (q + 1) * 128, rr * 128 : (rr + 1) * 128]
            low, high = swap_halves(tile[:64], tile[64:])
            y[4 * q + rr] = low.astype(BF16)
            y[16 + 4 * q + rr] = high.astype(BF16)


def gradient_kernel(y, table, windows, intensity, out, total):
    sign = lane_sign((128, 128))
    lefts = []
    for g in range(4):
        tiles = [y[:, n, g * 16 : (g + 1) * 16, :].astype(F32) for n in range(2)]
        for half in range(2):
            part = slice(half * 8, (half + 1) * 8)
            for u in swap_rows(tiles[0][:, part], tiles[1][:, part]):
                u = u.reshape(128, 128)
                lefts.append(jnp.concatenate([u, sign * pltpu.roll(u, 64, 1)], axis=0).astype(BF16))
    for n in range(4):
        cols = slice(n * 256, (n + 1) * 256)
        real = imag = 0.0
        for g in range(4):
            left = jnp.concatenate(lefts[4 * g : 4 * g + 4], axis=1)
            v = lax.dot_general(left, table[:, cols], TN, preferred_element_type=F32)
            for m in range(4):
                vr, vi = v[m * 128 : m * 128 + 64], v[m * 128 + 64 : m * 128 + 128]
                w = windows[4 * g + m, :, cols].astype(F32)
                wr, wi = w[:64], w[64:]
                real = real + (wr * vr + wi * vi)
                imag = imag + (wr * vi - wi * vr)
        total[0:64, cols] = real
        total[64:128, cols] = imag

    for t in range(8):
        cols = slice(t * 128, (t + 1) * 128)
        real = total[0:32, cols] + total[32:64, cols]
        imag = total[64:96, cols] + total[96:128, cols]
        turned = jnp.concatenate([real, imag], axis=0).T
        for n in range(2):
            both = jnp.concatenate([turned[n * 64 : n * 64 + 32], turned[n * 64 + 32 : n * 64 + 64]], axis=1)
            out[2 * t + n, 0:32] = both.astype(BF16)
    power = intensity[...]
    coarse = power.astype(BF16).astype(F32)
    out[:, 32:48] = jnp.concatenate([coarse, power - coarse], axis=1).astype(BF16)


def final_kernel(parts, grad, image):
    for yl in range(2):
        total = jnp.sum(
            jnp.stack([parts[2 * z + yl, 0:32].astype(F32) for z in range(NZ)]), axis=0
        )
        for h in range(2):
            for c in range(2):
                start = h * 64 + c * 32
                grad[c, h * 32 : (h + 1) * 32, yl * 32 : (yl + 1) * 32] = total[:, start : start + 32]
    for j in range(16):
        both = parts[j, 32:48].astype(F32)
        power = both[:8] + both[8:]
        for h in range(2):
            image[4 * j : 4 * j + 4, h * 128 : (h + 1) * 128] = power[4 * h : 4 * h + 4]


def vmem(count):
    return [pl.BlockSpec(memory_space=pltpu.VMEM)] * count


HBM = pl.BlockSpec(memory_space=pltpu.HBM)
ANY = pl.BlockSpec(memory_space=pl.ANY)
SMEM = pl.BlockSpec(memory_space=pltpu.SMEM)
SMALL = pltpu.CompilerParams(vmem_limit_bytes=6 * 1024 * 1024)
PARAMS = pltpu.CompilerParams(vmem_limit_bytes=VMEM_LIMIT)


def kept(array):
    return pltpu.with_memory_space_constraint(array, pltpu.VMEM)


def own_kernel(shifts, weights, out):
    place = lax.broadcasted_iota(jnp.int32, (16, 128), 1)
    column = ((lax.broadcasted_iota(jnp.int32, (16, 128), 0) & 1) * 32).astype(F32)
    own = column
    for m in range(2):
        own = jnp.where(place == 3 * m, shifts[m, 0].astype(F32), own)
        own = jnp.where(place == 3 * m + 1, shifts[m, 1].astype(F32) + column, own)
        own = jnp.where(place == 3 * m + 2, jnp.sqrt(jnp.full((16, 128), weights[m])), own)
    out[:, 0, :] = own


def own_call(shifts, weights):
    return pl.pallas_call(
        own_kernel,
        out_shape=jax.ShapeDtypeStruct((16, 1, 128), F32),
        in_specs=[SMEM, SMEM],
        out_specs=vmem(1)[0],
        name="own",
    )(shifts, weights)


def stage_call(place, here, pupil, measured):
    return pl.pallas_call(
        stage_kernel,
        out_shape=(
            pltpu.VMEM((2, 9, 64, 128), F32),
            pltpu.VMEM((2, 8, 32, 128), F32),
            pltpu.VMEM((8, NC), F32),
        ),
        in_specs=[SMEM] + vmem(2) + [HBM],
        out_specs=tuple(vmem(3)),
        scratch_shapes=[pltpu.VMEM((8, NC), F32), pltpu.SemaphoreType.DMA],
        compiler_params=SMALL,
        name="stage",
    )(place, here, pupil, pltpu.with_memory_space_constraint(measured, pltpu.HBM))


def rows_call(scal, table, here, beyond, share):
    far = pltpu.with_memory_space_constraint(jnp.asarray(col_tables()), pltpu.HBM)
    return pl.pallas_call(
        rows_kernel,
        out_shape=(
            jax.ShapeDtypeStruct((16, 2, 64, 128), BF16),
            pltpu.VMEM((16, 128, K), BF16),
            pltpu.VMEM((128, 128), F32),
            pltpu.VMEM((4, 512, 1024), BF16),
        ),
        in_specs=[ANY] + vmem(4) + [HBM],
        out_specs=tuple(vmem(4)),
        scratch_shapes=[
            pltpu.SMEM((16, 1, 128), F32),
            pltpu.VMEM((2, 9, 128, 128), F32),
            pltpu.VMEM((4, 512, K), BF16),
            pltpu.SemaphoreType.DMA,
            pltpu.SemaphoreType.DMA,
        ],
        compiler_params=PARAMS,
        name="rows",
    )(scal, kept(table), kept(here), kept(beyond), kept(share), far)


def image_call(x, table, measured, roots):
    return pl.pallas_call(
        image_kernel,
        out_shape=(
            jax.ShapeDtypeStruct((DEST, 64, 128), BF16),
            pltpu.VMEM((16, 8, 128), F32),
        ),
        in_specs=vmem(5),
        out_specs=tuple(vmem(2)),
        scratch_shapes=[
            pltpu.VMEM((4, 256, 512), BF16),
            pltpu.VMEM((4, 256, 1024), BF16),
            pltpu.VMEM((4, 128, 512), BF16),
        ],
        compiler_params=PARAMS,
        name="image",
    )(x, kept(jnp.asarray(lane_order())), kept(table), kept(measured), kept(roots))


def gradient_call(y, table, windows, intensity):
    return pl.pallas_call(
        gradient_kernel,
        out_shape=jax.ShapeDtypeStruct((16, 48, 128), BF16),
        in_specs=vmem(4),
        out_specs=vmem(1)[0],
        scratch_shapes=[pltpu.VMEM((128, K), F32)],
        compiler_params=PARAMS,
        name="gradient",
    )(y.reshape(16, 2, 64, 128), kept(table), kept(windows), kept(intensity))


def final_call(parts):
    return pl.pallas_call(
        final_kernel,
        out_shape=(jax.ShapeDtypeStruct((2, 64, 64), F32), jax.ShapeDtypeStruct((64, 256), F32)),
        in_specs=vmem(1),
        out_specs=tuple(vmem(2)),
        compiler_params=SMALL,
        name="final",
    )(kept(parts))


def exchange(blocks, axes):
    return lax.all_to_all(blocks, axes, split_axis=0, concat_axis=0, tiled=True)


def shards(pupil, mask_spectrum, shifts, weights, measured):
    z, yl = lax.axis_index("z"), lax.axis_index("yl")
    mask = mask_spectrum.transpose(0, 2, 1)
    own, late = lax.optimization_barrier((own_call(shifts, weights), mask))
    scal = exchange(own, ("z", "yl"))
    beyond = lax.ppermute(late, "row", [(i + 1, i) for i in range(NROW - 1)])
    place = jnp.stack([z, yl]).astype(jnp.int32)
    here, share, four = stage_call(place, mask, pupil.transpose(0, 2, 1), measured)
    table = lax.dynamic_index_in_dim(jnp.asarray(row_tables()), z, 0, keepdims=False)
    blocks, windows, roots, near = rows_call(scal, table, here, beyond, share)
    blocks, intensity = image_call(exchange(blocks.reshape(DEST, 64, 128), ("yl", "row")), near, four, roots)
    blocks = exchange(blocks, ("yl", "row"))
    parts = exchange(gradient_call(blocks, table, windows, intensity), ("z", "yl"))
    return final_call(parts)


def solution(mesh):
    finer = Mesh(mesh.devices.reshape(NZ, NYL, NROW), ("z", "yl", "row"))
    src = ("z", "yl")
    return jax.shard_map(
        shards,
        mesh=finer,
        in_specs=(
            P(None, None, "row"),
            P(None, None, "row"),
            P(src, None),
            P(src),
            P("row", None),
        ),
        out_specs=(P(None, src, "row"), P("row", src)),
        check_vma=False,
    )
```

```python
import functools
import math

import jax
import jax.numpy as jnp
import ml_dtypes
import numpy as np
from jax import lax
from jax.experimental import pallas as pl
from jax.experimental.pallas import tpu as pltpu
from jax.sharding import Mesh, PartitionSpec as P

K = 1024
NC = 4096
NR = 1024
SOURCES = 32
SH = 64
NZ = 8
NYL = 2
NROW = 16
DEST = NYL * NROW
GRAD_SCALE = 2.0 / math.sqrt(SOURCES * NR * NC)
VMEM_LIMIT = 20 * 1024 * 1024
F32 = jnp.float32
BF16 = jnp.bfloat16
NT = (((1,), (1,)), ((), ()))
TN = (((0,), (0,)), ((), ()))


def phase(position, frequency):
    turns = np.mod(position * frequency, NC).astype(np.float32)
    angle = turns * np.float32(2.0 * math.pi / NC)
    return np.cos(angle), np.sin(angle)


@functools.cache
def row_tables():
    z, yl, row, i = np.meshgrid(np.arange(NZ), np.arange(NYL), np.arange(NROW), np.arange(4), indexing="ij")
    x = (64 * row + 8 * z + 4 * yl + i).reshape(NZ, 128, 1)
    cosine, sine = phase(x, np.arange(K) - K // 2)
    return np.concatenate([cosine, sine], axis=1).astype(ml_dtypes.bfloat16)


@functools.cache
def col_tables():
    f0, q, rr, k1 = np.meshgrid(np.arange(4), np.arange(4), np.arange(4), np.arange(16), indexing="ij")
    f = (64 * (4 * q + rr) + 4 * k1 + f0 - K // 2).reshape(4, 4, 64, 1)
    cosine, sine = phase(f, np.arange(1024))
    return np.stack([cosine, sine], axis=2).reshape(4, 512, 1024).astype(ml_dtypes.bfloat16)


@functools.cache
def lane_order():
    rr, c, k = np.meshgrid(np.arange(4), np.arange(2), np.arange(64), indexing="ij")
    target = (k % 4) * 128 + c * 64 + rr * 16 + k // 4
    order = np.zeros((512, 512), np.float32)
    order[np.arange(512), target.reshape(-1)] = 1.0
    return order.astype(ml_dtypes.bfloat16)


def lane_sign(shape):
    lane = lax.broadcasted_iota(jnp.int32, shape, len(shape) - 1)
    return jnp.where((lane & 127) < 64, 1.0, -1.0).astype(F32)


def root_columns(low, high):
    lane = lax.broadcasted_iota(jnp.int32, (128, 128), 1)
    return jnp.where((lane & 32) == 0, low, high)


def swap_rows(a, b):
    low = lax.broadcasted_iota(jnp.int32, a.shape, 1) < 4
    return jnp.where(low, a, pltpu.roll(b, 4, 1)), jnp.where(low, pltpu.roll(a, 4, 1), b)


def stage_kernel(place, here, pupil, measured, mask, share, four, eight, arrived):
    rows = pl.ds(pl.multiple_of(place[0] * 8, 8), 8)
    copy = pltpu.make_async_copy(measured.at[rows, :], eight, arrived)
    copy.start()
    first = pl.multiple_of(place[1] * 32, 32)
    for c in range(2):
        for t in range(9):
            width = 128 if t < 8 else SH
            mask[c, t, :, :width] = here[c, :, t * 128 : t * 128 + width].astype(F32)
        for t in range(8):
            share[c, t] = pupil[c, pl.ds(first, 32), t * 128 : (t + 1) * 128]
    copy.wait()
    upper = lax.broadcasted_iota(jnp.int32, (8, NC), 0) >= 4
    wanted = upper == (place[1] == 1)
    four[...] = jnp.where(wanted, eight[...], pltpu.roll(eight[...], 4, 0))


def rows_kernel(
    gathered, table, here, beyond, share, far, out, windows, roots, near, scal, mask, fields, arrived, loaded
):
    copy = pltpu.make_async_copy(gathered, scal, arrived)
    copy.start()
    load = pltpu.make_async_copy(far, near, loaded)
    load.start()
    for c in range(2):
        for t in range(9):
            width = 128 if t < 8 else SH
            mask[c, t, 0:64, :width] = here[c, t, :, :width]
            mask[c, t, 64:128, :width] = beyond[c, :, t * 128 : t * 128 + width].astype(F32)
    copy.wait()
    for m in range(2):
        for p in range(16):
            at = m * 64 + p * 4
            roots[at : at + 4, :] = jnp.full((4, 128), scal[p, 0, 3 * m + 2])
    lane = lax.broadcasted_iota(jnp.int32, (32, 128), 1)
    sign = -lane_sign((128, 128))

    def build(p, field, at):
        first = [scal[p, 0, 3 * m + 1].astype(jnp.int32) for m in range(2)]
        by = [scal[p, 0, 3 * m].astype(jnp.int32) for m in range(2)]
        turn = [(128 - a) & 127 for a in by]
        keep = [lane < 128 - a for a in by]

        def turned(c, t, m):
            return pltpu.roll(mask[c, t, pl.ds(first[m], 32), :].astype(BF16), turn[m], 1)

        before = [[turned(c, 0, m) for c in range(2)] for m in range(2)]
        for t in range(8):
            cols = slice(t * 128, (t + 1) * 128)
            pr, pi = share[0, t], share[1, t]
            for m in range(2):
                after = [turned(c, t + 1, m) for c in range(2)]
                parts = [jnp.where(keep[m], before[m][c], after[c]) for c in range(2)]
                wr, wi = [part.astype(F32) for part in parts]
                before[m] = after
                low, high = m * 32, 64 + m * 32
                field[at + low : at + low + 32, cols] = (pr * wr - pi * wi).astype(BF16)
                field[at + high : at + high + 32, cols] = (pr * wi + pi * wr).astype(BF16)
                windows[p, low : low + 32, cols] = parts[0]
                windows[p, high : high + 32, cols] = parts[1]

    def transform(g, field):
        mixed = []
        for half in range(2):
            rows = field[half * 256 : (half + 1) * 256, :]
            both = lax.dot_general(table[...], rows, NT, preferred_element_type=F32)
            for n in range(2):
                p = 4 * g + 2 * half + n
                by_cos = both[:128, n * 128 : (n + 1) * 128]
                by_sin = both[128:, n * 128 : (n + 1) * 128]
                root = root_columns(scal[p, 0, 2], scal[p, 0, 5]) * (1.0 / K)
                mixed.append(((by_cos + sign * pltpu.roll(by_sin, 64, 1)) * root).reshape(16, 8, 128))
        first, second = swap_rows(mixed[0], mixed[1]), swap_rows(mixed[2], mixed[3])
        for n in range(2):
            tile = jnp.concatenate([first[n], second[n]], axis=1).astype(BF16)
            out[:, n, g * 16 : (g + 1) * 16, :] = tile

    for g in range(5):
        if g < 4:
            for n in range(4):
                build(4 * g + n, fields.at[g], n * 128)
        if g > 0:
            transform(g - 1, fields.at[g - 1])
    load.wait()


def swap_halves(a, b):
    low = (lax.broadcasted_iota(jnp.int32, a.shape, 1) & 32) == 0
    return jnp.where(low, a, pltpu.roll(b, 32, 1)), jnp.where(low, pltpu.roll(a, 96, 1), b)


def image_kernel(x, order, table, measured, roots, y, intensity, left, back, parts):
    sign = lane_sign((128, 128))
    stacked = []
    for q in range(4):
        tiles = []
        for rr in range(4):
            r = 4 * q + rr
            tiles.append(jnp.concatenate(swap_halves(x[r], x[16 + r]), axis=0))
        stacked.append(jnp.concatenate(tiles, axis=1))
    sorted_lanes = jnp.dot(jnp.concatenate(stacked, axis=0), order[...], preferred_element_type=F32)
    for q in range(4):
        for f0 in range(4):
            tile = sorted_lanes[q * 128 : (q + 1) * 128, f0 * 128 : (f0 + 1) * 128]
            left[f0, 0:128, q * 128 : (q + 1) * 128] = (tile * sign).astype(BF16)
            left[f0, 128:256, q * 128 : (q + 1) * 128] = pltpu.roll(tile.astype(BF16), 64, 1)

    upper = lax.broadcasted_iota(jnp.int32, (8, 128), 0) < 4
    for n in range(4):
        cols = slice(n * 256, (n + 1) * 256)
        h = [jnp.dot(left[f0], table[f0, :, cols], preferred_element_type=F32) for f0 in range(4)]
        s02, d02, s13, d13 = h[0] + h[2], h[0] - h[2], h[1] + h[3], h[1] - h[3]
        turned = jnp.concatenate([-d13[128:], d13[:128]], axis=0)
        fields = [s02 + s13, d02 + turned, s02 - s13, d02 - turned]
        scaled = []
        for y1 in range(4):
            e = fields[y1].reshape(2, 16, 8, 256)
            power = jnp.sum(e[0] * e[0] + e[1] * e[1], axis=0)
            power = (power + pltpu.roll(power, 4, 0)) * (1.0 / SOURCES)
            intensity[y1 * 4 + n] = jnp.where(upper, power[:, :128], power[:, 128:])
            residual = power - measured[:, y1 * 1024 + n * 256 : y1 * 1024 + (n + 1) * 256]
            scaled.append((e * (residual * GRAD_SCALE)[None, None]).reshape(256, 256))
        s02, d02 = scaled[0] + scaled[2], scaled[0] - scaled[2]
        s13, d13 = scaled[1] + scaled[3], scaled[1] - scaled[3]
        turned = jnp.concatenate([-d13[128:], d13[:128]], axis=0)
        back[0, :, cols] = (s02 + s13).astype(BF16)
        back[1, :, cols] = (d02 - turned).astype(BF16)
        back[2, :, cols] = (s02 - s13).astype(BF16)
        back[3, :, cols] = (d02 + turned).astype(BF16)

    for f0 in range(4):
        both = lax.dot_general(back[f0], table[f0], NT, preferred_element_type=F32)
        for q in range(4):
            cols = slice(q * 128, (q + 1) * 128)
            mixed = sign * both[:128, cols] + pltpu.roll(both[128:, cols], 64, 1)
            parts[q, :, f0 * 128 : (f0 + 1) * 128] = (mixed * roots[...]).astype(BF16)
    lined = lax.dot_general(parts[...].reshape(512, 512), order[...], NT, preferred_element_type=F32)
    for q in range(4):
        for rr in range(4):
            tile = lined[q * 128 : (q + 1) * 128, rr * 128 : (rr + 1) * 128].astype(BF16)
            y[4 * q + rr], y[16 + 4 * q + rr] = swap_halves(tile[:64], tile[64:])


def gradient_kernel(y, table, windows, intensity, out, total):
    sign = lane_sign((128, 128)).astype(BF16)
    lefts = []
    for g in range(4):
        tiles = [y[:, n, g * 16 : (g + 1) * 16, :].astype(F32) for n in range(2)]
        for half in range(2):
            part = slice(half * 8, (half + 1) * 8)
            for u in swap_rows(tiles[0][:, part], tiles[1][:, part]):
                u = u.reshape(128, 128).astype(BF16)
                lefts.append(jnp.concatenate([u, sign * pltpu.roll(u, 64, 1)], axis=0))
    for n in range(4):
        cols = slice(n * 256, (n + 1) * 256)
        real = imag = 0.0
        for g in range(4):
            left = jnp.concatenate(lefts[4 * g : 4 * g + 4], axis=1)
            v = lax.dot_general(left, table[:, cols], TN, preferred_element_type=F32)
            for m in range(4):
                vr, vi = v[m * 128 : m * 128 + 64], v[m * 128 + 64 : m * 128 + 128]
                w = windows[4 * g + m, :, cols].astype(F32)
                wr, wi = w[:64], w[64:]
                real = real + (wr * vr + wi * vi)
                imag = imag + (wr * vi - wi * vr)
        total[0:64, cols] = real
        total[64:128, cols] = imag

    for t in range(8):
        cols = slice(t * 128, (t + 1) * 128)
        real = total[0:32, cols] + total[32:64, cols]
        imag = total[64:96, cols] + total[96:128, cols]
        turned = jnp.concatenate([real, imag], axis=0).T
        for n in range(2):
            both = jnp.concatenate([turned[n * 64 : n * 64 + 32], turned[n * 64 + 32 : n * 64 + 64]], axis=1)
            out[2 * t + n, 0:4] = both.reshape(4, 8, 128).astype(BF16)
    out[:, 4] = intensity[...].astype(BF16)


def final_kernel(parts, grad, image):
    for yl in range(2):
        total = jnp.sum(
            jnp.stack([parts[2 * z + yl, 0:4].astype(F32).reshape(32, 128) for z in range(NZ)]), axis=0
        )
        for h in range(2):
            for c in range(2):
                start = h * 64 + c * 32
                grad[c, h * 32 : (h + 1) * 32, yl * 32 : (yl + 1) * 32] = total[:, start : start + 32]
    for j in range(16):
        power = parts[j, 4].astype(F32)
        for h in range(2):
            image[4 * j : 4 * j + 4, h * 128 : (h + 1) * 128] = power[4 * h : 4 * h + 4]


def vmem(count):
    return [pl.BlockSpec(memory_space=pltpu.VMEM)] * count


HBM = pl.BlockSpec(memory_space=pltpu.HBM)
ANY = pl.BlockSpec(memory_space=pl.ANY)
SMEM = pl.BlockSpec(memory_space=pltpu.SMEM)
SMALL = pltpu.CompilerParams(vmem_limit_bytes=6 * 1024 * 1024)
PARAMS = pltpu.CompilerParams(vmem_limit_bytes=VMEM_LIMIT)


def kept(array):
    return pltpu.with_memory_space_constraint(array, pltpu.VMEM)


def own_kernel(shifts, weights, out):
    place = lax.broadcasted_iota(jnp.int32, (16, 128), 1)
    column = ((lax.broadcasted_iota(jnp.int32, (16, 128), 0) & 1) * 32).astype(F32)
    own = column
    for m in range(2):
        own = jnp.where(place == 3 * m, shifts[m, 0].astype(F32), own)
        own = jnp.where(place == 3 * m + 1, shifts[m, 1].astype(F32) + column, own)
        own = jnp.where(place == 3 * m + 2, jnp.sqrt(jnp.full((16, 128), weights[m])), own)
    out[:, 0, :] = own


def own_call(shifts, weights):
    return pl.pallas_call(
        own_kernel,
        out_shape=pltpu.VMEM((16, 1, 128), F32),
        in_specs=[SMEM, SMEM],
        out_specs=vmem(1)[0],
        name="own",
    )(shifts, weights)


def stage_call(place, here, pupil, measured):
    return pl.pallas_call(
        stage_kernel,
        out_shape=(
            pltpu.VMEM((2, 9, 64, 128), F32),
            pltpu.VMEM((2, 8, 32, 128), F32),
            pltpu.VMEM((8, NC), F32),
        ),
        in_specs=[SMEM] + vmem(2) + [HBM],
        out_specs=tuple(vmem(3)),
        scratch_shapes=[pltpu.VMEM((8, NC), F32), pltpu.SemaphoreType.DMA],
        compiler_params=SMALL,
        name="stage",
    )(place, here, pupil, pltpu.with_memory_space_constraint(measured, pltpu.HBM))


def rows_call(scal, table, here, beyond, share):
    far = pltpu.with_memory_space_constraint(jnp.asarray(col_tables()), pltpu.HBM)
    return pl.pallas_call(
        rows_kernel,
        out_shape=(
            jax.ShapeDtypeStruct((16, 2, 64, 128), BF16),
            pltpu.VMEM((16, 128, K), BF16),
            pltpu.VMEM((128, 128), F32),
            pltpu.VMEM((4, 512, 1024), BF16),
        ),
        in_specs=[ANY] + vmem(4) + [HBM],
        out_specs=tuple(vmem(4)),
        scratch_shapes=[
            pltpu.SMEM((16, 1, 128), F32),
            pltpu.VMEM((2, 9, 128, 128), F32),
            pltpu.VMEM((4, 512, K), BF16),
            pltpu.SemaphoreType.DMA,
            pltpu.SemaphoreType.DMA,
        ],
        compiler_params=PARAMS,
        name="rows",
    )(scal, kept(table), kept(here), kept(beyond), kept(share), far)


def image_call(x, table, measured, roots):
    return pl.pallas_call(
        image_kernel,
        out_shape=(
            jax.ShapeDtypeStruct((DEST, 64, 128), BF16),
            pltpu.VMEM((16, 8, 128), F32),
        ),
        in_specs=vmem(5),
        out_specs=tuple(vmem(2)),
        scratch_shapes=[
            pltpu.VMEM((4, 256, 512), BF16),
            pltpu.VMEM((4, 256, 1024), BF16),
            pltpu.VMEM((4, 128, 512), BF16),
        ],
        compiler_params=PARAMS,
        name="image",
    )(x, kept(jnp.asarray(lane_order())), kept(table), kept(measured), kept(roots))


def gradient_call(y, table, windows, intensity):
    return pl.pallas_call(
        gradient_kernel,
        out_shape=jax.ShapeDtypeStruct((16, 5, 8, 128), BF16),
        in_specs=vmem(4),
        out_specs=vmem(1)[0],
        scratch_shapes=[pltpu.VMEM((128, K), F32)],
        compiler_params=PARAMS,
        name="gradient",
    )(y.reshape(16, 2, 64, 128), kept(table), kept(windows), kept(intensity))


def final_call(parts):
    return pl.pallas_call(
        final_kernel,
        out_shape=(jax.ShapeDtypeStruct((2, 64, 64), F32), jax.ShapeDtypeStruct((64, 256), F32)),
        in_specs=vmem(1),
        out_specs=tuple(vmem(2)),
        compiler_params=SMALL,
        name="final",
    )(kept(parts))


def exchange(blocks, axes):
    return lax.all_to_all(blocks, axes, split_axis=0, concat_axis=0, tiled=True)


def shards(pupil, mask_spectrum, shifts, weights, measured):
    z, yl = lax.axis_index("z"), lax.axis_index("yl")
    mask = mask_spectrum.transpose(0, 2, 1)
    scal = exchange(own_call(shifts, weights), ("z", "yl"))
    beyond = lax.ppermute(mask, "row", [(i + 1, i) for i in range(NROW - 1)])
    place = jnp.stack([z, yl]).astype(jnp.int32)
    here, share, four = stage_call(place, mask, pupil.transpose(0, 2, 1), measured)
    table = lax.dynamic_index_in_dim(jnp.asarray(row_tables()), z, 0, keepdims=False)
    blocks, windows, roots, near = rows_call(scal, table, here, beyond, share)
    blocks, intensity = image_call(exchange(blocks.reshape(DEST, 64, 128), ("yl", "row")), near, four, roots)
    blocks = exchange(blocks, ("yl", "row"))
    parts = exchange(gradient_call(blocks, table, windows, intensity), ("z", "yl"))
    return final_call(parts)


def solution(mesh):
    finer = Mesh(mesh.devices.reshape(NZ, NYL, NROW), ("z", "yl", "row"))
    src = ("z", "yl")
    return jax.shard_map(
        shards,
        mesh=finer,
        in_specs=(
            P(None, None, "row"),
            P(None, None, "row"),
            P(src, None),
            P(src),
            P("row", None),
        ),
        out_specs=(P(None, src, "row"), P("row", src)),
        check_vma=False,
    )
```

```python
import functools
import math

import jax
import jax.numpy as jnp
import ml_dtypes
import numpy as np
from jax import lax
from jax.experimental import pallas as pl
from jax.experimental.pallas import tpu as pltpu
from jax.sharding import Mesh, PartitionSpec as P

K = 1024
NC = 4096
NR = 1024
SOURCES = 32
SH = 64
NZ = 8
NYL = 2
NROW = 16
DEST = NYL * NROW
GRAD_SCALE = 2.0 / math.sqrt(SOURCES * NR * NC)
VMEM_LIMIT = 20 * 1024 * 1024
F32 = jnp.float32
BF16 = jnp.bfloat16
NT = (((1,), (1,)), ((), ()))
TN = (((0,), (0,)), ((), ()))


def phase(position, frequency):
    turns = np.mod(position * frequency, NC).astype(np.float32)
    angle = turns * np.float32(2.0 * math.pi / NC)
    return np.cos(angle), np.sin(angle)


@functools.cache
def row_tables():
    z, yl, row, i = np.meshgrid(np.arange(NZ), np.arange(NYL), np.arange(NROW), np.arange(4), indexing="ij")
    x = (64 * row + 8 * z + 4 * yl + i).reshape(NZ, 128, 1)
    cosine, sine = phase(x, np.arange(K) - K // 2)
    return np.concatenate([cosine, sine], axis=1).astype(ml_dtypes.bfloat16)


@functools.cache
def col_tables():
    f0, q, rr, k1 = np.meshgrid(np.arange(4), np.arange(4), np.arange(4), np.arange(16), indexing="ij")
    f = (64 * (4 * q + rr) + 4 * k1 + f0 - K // 2).reshape(4, 4, 64, 1)
    cosine, sine = phase(f, np.arange(1024))
    return np.stack([cosine, sine], axis=2).reshape(4, 512, 1024).astype(ml_dtypes.bfloat16)


@functools.cache
def lane_order():
    rr, c, k = np.meshgrid(np.arange(4), np.arange(2), np.arange(64), indexing="ij")
    target = (k % 4) * 128 + c * 64 + rr * 16 + k // 4
    order = np.zeros((512, 512), np.float32)
    order[np.arange(512), target.reshape(-1)] = 1.0
    return order.astype(ml_dtypes.bfloat16)


def lane_sign(shape):
    lane = lax.broadcasted_iota(jnp.int32, shape, len(shape) - 1)
    return jnp.where((lane & 127) < 64, 1.0, -1.0).astype(F32)


def root_columns(low, high):
    lane = lax.broadcasted_iota(jnp.int32, (128, 128), 1)
    return jnp.where((lane & 32) == 0, low, high)


def swap_rows(a, b):
    low = lax.broadcasted_iota(jnp.int32, a.shape, 1) < 4
    return jnp.where(low, a, pltpu.roll(b, 4, 1)), jnp.where(low, pltpu.roll(a, 4, 1), b)


def stage_kernel(place, here, pupil, measured, mask, share, four, eight, arrived):
    rows = pl.ds(pl.multiple_of(place[0] * 8, 8), 8)
    copy = pltpu.make_async_copy(measured.at[rows, :], eight, arrived)
    copy.start()
    first = pl.multiple_of(place[1] * 32, 32)
    for c in range(2):
        for t in range(9):
            width = 128 if t < 8 else SH
            mask[c, t, :, :width] = here[c, :, t * 128 : t * 128 + width].astype(F32)
        for t in range(8):
            share[c, t] = pupil[c, pl.ds(first, 32), t * 128 : (t + 1) * 128]
    copy.wait()
    upper = lax.broadcasted_iota(jnp.int32, (8, NC), 0) >= 4
    wanted = upper == (place[1] == 1)
    four[...] = jnp.where(wanted, eight[...], pltpu.roll(eight[...], 4, 0))


def rows_kernel(
    gathered, table, here, beyond, share, far, out, windows, roots, near, scal, mask, fields, arrived, loaded
):
    copy = pltpu.make_async_copy(gathered, scal, arrived)
    copy.start()
    load = pltpu.make_async_copy(far, near, loaded)
    load.start()
    for c in range(2):
        for t in range(9):
            width = 128 if t < 8 else SH
            mask[c, t, 0:64, :width] = here[c, t, :, :width]
            mask[c, t, 64:128, :width] = beyond[c, :, t * 128 : t * 128 + width].astype(F32)
    copy.wait()
    for m in range(2):
        for p in range(16):
            at = m * 64 + p * 4
            roots[at : at + 4, :] = jnp.full((4, 128), scal[p, 0, 3 * m + 2])
    lane = lax.broadcasted_iota(jnp.int32, (32, 128), 1)
    sign = -lane_sign((128, 128))

    def build(p, field, at):
        first = [scal[p, 0, 3 * m + 1].astype(jnp.int32) for m in range(2)]
        by = [scal[p, 0, 3 * m].astype(jnp.int32) for m in range(2)]
        turn = [(128 - a) & 127 for a in by]
        keep = [lane < 128 - a for a in by]

        def turned(c, t, m):
            return pltpu.roll(mask[c, t, pl.ds(first[m], 32), :].astype(BF16), turn[m], 1)

        before = [[turned(c, 0, m) for c in range(2)] for m in range(2)]
        for t in range(8):
            cols = slice(t * 128, (t + 1) * 128)
            pr, pi = share[0, t], share[1, t]
            for m in range(2):
                after = [turned(c, t + 1, m) for c in range(2)]
                parts = [jnp.where(keep[m], before[m][c], after[c]) for c in range(2)]
                wr, wi = [part.astype(F32) for part in parts]
                before[m] = after
                low, high = m * 32, 64 + m * 32
                field[at + low : at + low + 32, cols] = (pr * wr - pi * wi).astype(BF16)
                field[at + high : at + high + 32, cols] = (pr * wi + pi * wr).astype(BF16)
                windows[p, low : low + 32, cols] = parts[0]
                windows[p, high : high + 32, cols] = parts[1]

    def transform(g, field):
        mixed = []
        for half in range(2):
            rows = field[half * 256 : (half + 1) * 256, :]
            both = lax.dot_general(table[...], rows, NT, preferred_element_type=F32)
            for n in range(2):
                p = 4 * g + 2 * half + n
                by_cos = both[:128, n * 128 : (n + 1) * 128]
                by_sin = both[128:, n * 128 : (n + 1) * 128]
                root = root_columns(scal[p, 0, 2], scal[p, 0, 5]) * (1.0 / K)
                mixed.append(((by_cos + sign * pltpu.roll(by_sin, 64, 1)) * root).reshape(16, 8, 128))
        first, second = swap_rows(mixed[0], mixed[1]), swap_rows(mixed[2], mixed[3])
        for n in range(2):
            tile = jnp.concatenate([first[n], second[n]], axis=1).astype(BF16)
            out[:, n, g * 16 : (g + 1) * 16, :] = tile

    for g in range(5):
        if g < 4:
            for n in range(4):
                build(4 * g + n, fields.at[g], n * 128)
        if g > 0:
            transform(g - 1, fields.at[g - 1])
    load.wait()


def swap_halves(a, b):
    low = (lax.broadcasted_iota(jnp.int32, a.shape, 1) & 32) == 0
    return jnp.where(low, a, pltpu.roll(b, 32, 1)), jnp.where(low, pltpu.roll(a, 96, 1), b)


def image_kernel(x, order, table, measured, roots, y, intensity, left, back, parts):
    sign = lane_sign((128, 128))
    stacked = []
    for q in range(4):
        tiles = []
        for rr in range(4):
            r = 4 * q + rr
            tiles.append(jnp.concatenate(swap_halves(x[r], x[16 + r]), axis=0))
        stacked.append(jnp.concatenate(tiles, axis=1))
    sorted_lanes = jnp.dot(jnp.concatenate(stacked, axis=0), order[...], preferred_element_type=F32)
    for q in range(4):
        for f0 in range(4):
            tile = sorted_lanes[q * 128 : (q + 1) * 128, f0 * 128 : (f0 + 1) * 128]
            left[f0, 0:128, q * 128 : (q + 1) * 128] = (tile * sign).astype(BF16)
            left[f0, 128:256, q * 128 : (q + 1) * 128] = pltpu.roll(tile.astype(BF16), 64, 1)

    upper = lax.broadcasted_iota(jnp.int32, (8, 128), 0) < 4
    for n in range(4):
        cols = slice(n * 256, (n + 1) * 256)
        h = [jnp.dot(left[f0], table[f0, :, cols], preferred_element_type=F32) for f0 in range(4)]
        s02, d02, s13, d13 = h[0] + h[2], h[0] - h[2], h[1] + h[3], h[1] - h[3]
        turned = jnp.concatenate([-d13[128:], d13[:128]], axis=0)
        fields = [s02 + s13, d02 + turned, s02 - s13, d02 - turned]
        scaled = []
        for y1 in range(4):
            e = fields[y1].reshape(2, 16, 8, 256)
            power = jnp.sum(e[0] * e[0] + e[1] * e[1], axis=0)
            power = (power + pltpu.roll(power, 4, 0)) * (1.0 / SOURCES)
            intensity[y1 * 4 + n] = jnp.where(upper, power[:, :128], power[:, 128:])
            residual = power - measured[:, y1 * 1024 + n * 256 : y1 * 1024 + (n + 1) * 256]
            scaled.append((e * (residual * GRAD_SCALE)[None, None]).reshape(256, 256))
        s02, d02 = scaled[0] + scaled[2], scaled[0] - scaled[2]
        s13, d13 = scaled[1] + scaled[3], scaled[1] - scaled[3]
        turned = jnp.concatenate([-d13[128:], d13[:128]], axis=0)
        back[0, :, cols] = (s02 + s13).astype(BF16)
        back[1, :, cols] = (d02 - turned).astype(BF16)
        back[2, :, cols] = (s02 - s13).astype(BF16)
        back[3, :, cols] = (d02 + turned).astype(BF16)

    for f0 in range(4):
        both = lax.dot_general(back[f0], table[f0], NT, preferred_element_type=F32)
        for q in range(4):
            cols = slice(q * 128, (q + 1) * 128)
            mixed = sign * both[:128, cols] + pltpu.roll(both[128:, cols], 64, 1)
            parts[q, :, f0 * 128 : (f0 + 1) * 128] = (mixed * roots[...]).astype(BF16)
    lined = lax.dot_general(parts[...].reshape(512, 512), order[...], NT, preferred_element_type=F32)
    for q in range(4):
        for rr in range(4):
            tile = lined[q * 128 : (q + 1) * 128, rr * 128 : (rr + 1) * 128].astype(BF16)
            y[4 * q + rr], y[16 + 4 * q + rr] = swap_halves(tile[:64], tile[64:])


def gradient_kernel(y, table, windows, intensity, out, total):
    sign = lane_sign((128, 128)).astype(BF16)
    lefts = []
    for g in range(4):
        tiles = [y[:, n, g * 16 : (g + 1) * 16, :].astype(F32) for n in range(2)]
        for half in range(2):
            part = slice(half * 8, (half + 1) * 8)
            for u in swap_rows(tiles[0][:, part], tiles[1][:, part]):
                u = u.reshape(128, 128).astype(BF16)
                lefts.append(jnp.concatenate([u, sign * pltpu.roll(u, 64, 1)], axis=0))
    for n in range(4):
        cols = slice(n * 256, (n + 1) * 256)
        real = imag = 0.0
        for g in range(4):
            left = jnp.concatenate(lefts[4 * g : 4 * g + 4], axis=1)
            v = lax.dot_general(left, table[:, cols], TN, preferred_element_type=F32)
            for m in range(4):
                vr, vi = v[m * 128 : m * 128 + 64], v[m * 128 + 64 : m * 128 + 128]
                w = windows[4 * g + m, :, cols].astype(F32)
                wr, wi = w[:64], w[64:]
                real = real + (wr * vr + wi * vi)
                imag = imag + (wr * vi - wi * vr)
        total[0:64, cols] = real
        total[64:128, cols] = imag

    for t in range(8):
        cols = slice(t * 128, (t + 1) * 128)
        real = total[0:32, cols] + total[32:64, cols]
        imag = total[64:96, cols] + total[96:128, cols]
        turned = jnp.concatenate([real, imag], axis=0).T
        for n in range(2):
            both = jnp.concatenate([turned[n * 64 : n * 64 + 32], turned[n * 64 + 32 : n * 64 + 64]], axis=1)
            out[8 * n + t, 0:4] = both.reshape(4, 8, 128).astype(BF16)
    for yl in range(2):
        for z in range(8):
            out[8 * yl + z, 4] = intensity[2 * z + yl].astype(BF16)


def final_kernel(parts, grad, image):
    for yl in range(2):
        total = jnp.sum(
            jnp.stack([parts[8 * yl + z, 0:4].astype(F32).reshape(32, 128) for z in range(NZ)]), axis=0
        )
        for h in range(2):
            for c in range(2):
                start = h * 64 + c * 32
                grad[c, h * 32 : (h + 1) * 32, yl * 32 : (yl + 1) * 32] = total[:, start : start + 32]
    for j in range(16):
        power = parts[j % 2 * 8 + j // 2, 4].astype(F32)
        for h in range(2):
            image[4 * j : 4 * j + 4, h * 128 : (h + 1) * 128] = power[4 * h : 4 * h + 4]


def vmem(count):
    return [pl.BlockSpec(memory_space=pltpu.VMEM)] * count


HBM = pl.BlockSpec(memory_space=pltpu.HBM)
ANY = pl.BlockSpec(memory_space=pl.ANY)
SMEM = pl.BlockSpec(memory_space=pltpu.SMEM)
SMALL = pltpu.CompilerParams(vmem_limit_bytes=6 * 1024 * 1024)
PARAMS = pltpu.CompilerParams(vmem_limit_bytes=VMEM_LIMIT)


def kept(array):
    return pltpu.with_memory_space_constraint(array, pltpu.VMEM)


def own_kernel(shifts, weights, out):
    place = lax.broadcasted_iota(jnp.int32, (16, 128), 1)
    column = ((lax.broadcasted_iota(jnp.int32, (16, 128), 0) & 1) * 32).astype(F32)
    own = column
    for m in range(2):
        own = jnp.where(place == 3 * m, shifts[m, 0].astype(F32), own)
        own = jnp.where(place == 3 * m + 1, shifts[m, 1].astype(F32) + column, own)
        own = jnp.where(place == 3 * m + 2, jnp.sqrt(jnp.full((16, 128), weights[m])), own)
    out[:, 0, :] = own


def own_call(shifts, weights):
    return pl.pallas_call(
        own_kernel,
        out_shape=pltpu.VMEM((16, 1, 128), F32),
        in_specs=[SMEM, SMEM],
        out_specs=vmem(1)[0],
        name="own",
    )(shifts, weights)


def stage_call(place, here, pupil, measured):
    return pl.pallas_call(
        stage_kernel,
        out_shape=(
            pltpu.VMEM((2, 9, 64, 128), F32),
            pltpu.VMEM((2, 8, 32, 128), F32),
            pltpu.VMEM((8, NC), F32),
        ),
        in_specs=[SMEM] + vmem(2) + [HBM],
        out_specs=tuple(vmem(3)),
        scratch_shapes=[pltpu.VMEM((8, NC), F32), pltpu.SemaphoreType.DMA],
        compiler_params=SMALL,
        name="stage",
    )(place, here, pupil, pltpu.with_memory_space_constraint(measured, pltpu.HBM))


def rows_call(scal, table, here, beyond, share):
    far = pltpu.with_memory_space_constraint(jnp.asarray(col_tables()), pltpu.HBM)
    return pl.pallas_call(
        rows_kernel,
        out_shape=(
            jax.ShapeDtypeStruct((16, 2, 64, 128), BF16),
            pltpu.VMEM((16, 128, K), BF16),
            pltpu.VMEM((128, 128), F32),
            pltpu.VMEM((4, 512, 1024), BF16),
        ),
        in_specs=[ANY] + vmem(4) + [HBM],
        out_specs=tuple(vmem(4)),
        scratch_shapes=[
            pltpu.SMEM((16, 1, 128), F32),
            pltpu.VMEM((2, 9, 128, 128), F32),
            pltpu.VMEM((4, 512, K), BF16),
            pltpu.SemaphoreType.DMA,
            pltpu.SemaphoreType.DMA,
        ],
        compiler_params=PARAMS,
        name="rows",
    )(scal, kept(table), kept(here), kept(beyond), kept(share), far)


def image_call(x, table, measured, roots):
    return pl.pallas_call(
        image_kernel,
        out_shape=(
            jax.ShapeDtypeStruct((DEST, 64, 128), BF16),
            pltpu.VMEM((16, 8, 128), F32),
        ),
        in_specs=vmem(5),
        out_specs=tuple(vmem(2)),
        scratch_shapes=[
            pltpu.VMEM((4, 256, 512), BF16),
            pltpu.VMEM((4, 256, 1024), BF16),
            pltpu.VMEM((4, 128, 512), BF16),
        ],
        compiler_params=PARAMS,
        name="image",
    )(x, kept(jnp.asarray(lane_order())), kept(table), kept(measured), kept(roots))


def gradient_call(y, table, windows, intensity):
    return pl.pallas_call(
        gradient_kernel,
        out_shape=jax.ShapeDtypeStruct((16, 5, 8, 128), BF16),
        in_specs=vmem(4),
        out_specs=vmem(1)[0],
        scratch_shapes=[pltpu.VMEM((128, K), F32)],
        compiler_params=PARAMS,
        name="gradient",
    )(y.reshape(16, 2, 64, 128), kept(table), kept(windows), kept(intensity))


def final_call(parts):
    return pl.pallas_call(
        final_kernel,
        out_shape=(jax.ShapeDtypeStruct((2, 64, 64), F32), jax.ShapeDtypeStruct((64, 256), F32)),
        in_specs=vmem(1),
        out_specs=tuple(vmem(2)),
        compiler_params=SMALL,
        name="final",
    )(kept(parts))


def exchange(blocks, axes):
    return lax.all_to_all(blocks, axes, split_axis=0, concat_axis=0, tiled=True)


def shards(pupil, mask_spectrum, shifts, weights, measured):
    z, yl = lax.axis_index("z"), lax.axis_index("yl")
    mask = mask_spectrum.transpose(0, 2, 1)
    scal = exchange(own_call(shifts, weights), ("z", "yl"))
    beyond = lax.ppermute(mask, "row", [(i + 1, i) for i in range(NROW - 1)])
    place = jnp.stack([z, yl]).astype(jnp.int32)
    here, share, four = stage_call(place, mask, pupil.transpose(0, 2, 1), measured)
    table = lax.dynamic_index_in_dim(jnp.asarray(row_tables()), z, 0, keepdims=False)
    blocks, windows, roots, near = rows_call(scal, table, here, beyond, share)
    blocks, intensity = image_call(exchange(blocks.reshape(DEST, 64, 128), ("yl", "row")), near, four, roots)
    blocks = exchange(blocks, ("yl", "row"))
    parts = exchange(gradient_call(blocks, table, windows, intensity), ("yl", "z"))
    return final_call(parts)


def solution(mesh):
    finer = Mesh(mesh.devices.reshape(NZ, NYL, NROW), ("z", "yl", "row"))
    src = ("z", "yl")
    return jax.shard_map(
        shards,
        mesh=finer,
        in_specs=(
            P(None, None, "row"),
            P(None, None, "row"),
            P(src, None),
            P(src),
            P("row", None),
        ),
        out_specs=(P(None, src, "row"), P("row", src)),
        check_vma=False,
    )
```

```python
import functools
import math

import jax
import jax.numpy as jnp
import ml_dtypes
import numpy as np
from jax import lax
from jax.experimental import pallas as pl
from jax.experimental.pallas import tpu as pltpu
from jax.sharding import Mesh, PartitionSpec as P

K = 1024
NC = 4096
NR = 1024
SOURCES = 32
SH = 64
NZ = 8
NYL = 2
NROW = 16
DEST = NYL * NROW
GRAD_SCALE = 2.0 / math.sqrt(SOURCES * NR * NC)
VMEM_LIMIT = 20 * 1024 * 1024
F32 = jnp.float32
BF16 = jnp.bfloat16
NT = (((1,), (1,)), ((), ()))
TN = (((0,), (0,)), ((), ()))


def phase(position, frequency):
    turns = np.mod(position * frequency, NC).astype(np.float32)
    angle = turns * np.float32(2.0 * math.pi / NC)
    return np.cos(angle), np.sin(angle)


@functools.cache
def row_tables():
    z, row, yl, i = np.meshgrid(np.arange(NZ), np.arange(NROW), np.arange(NYL), np.arange(4), indexing="ij")
    x = (64 * row + 8 * z + 4 * yl + i).reshape(NZ, 128, 1)
    cosine, sine = phase(x, np.arange(K) - K // 2)
    return np.concatenate([cosine, sine], axis=1).astype(ml_dtypes.bfloat16)


@functools.cache
def col_tables():
    f0, q, rr, k1 = np.meshgrid(np.arange(4), np.arange(4), np.arange(4), np.arange(16), indexing="ij")
    f = (64 * (4 * q + rr) + 4 * k1 + f0 - K // 2).reshape(4, 4, 64, 1)
    cosine, sine = phase(f, np.arange(1024))
    return np.stack([cosine, sine], axis=2).reshape(4, 512, 1024).astype(ml_dtypes.bfloat16)


@functools.cache
def lane_order():
    rr, c, k = np.meshgrid(np.arange(4), np.arange(2), np.arange(64), indexing="ij")
    target = (k % 4) * 128 + c * 64 + rr * 16 + k // 4
    order = np.zeros((512, 512), np.float32)
    order[np.arange(512), target.reshape(-1)] = 1.0
    return order.astype(ml_dtypes.bfloat16)


def lane_sign(shape):
    lane = lax.broadcasted_iota(jnp.int32, shape, len(shape) - 1)
    return jnp.where((lane & 127) < 64, 1.0, -1.0).astype(F32)


def root_columns(low, high):
    lane = lax.broadcasted_iota(jnp.int32, (128, 128), 1)
    return jnp.where((lane & 32) == 0, low, high)


def swap_rows(a, b):
    low = lax.broadcasted_iota(jnp.int32, a.shape, 1) < 4
    return jnp.where(low, a, pltpu.roll(b, 4, 1)), jnp.where(low, pltpu.roll(a, 4, 1), b)


def stage_kernel(place, here, pupil, measured, mask, share, four, eight, arrived):
    rows = pl.ds(pl.multiple_of(place[0] * 8, 8), 8)
    copy = pltpu.make_async_copy(measured.at[rows, :], eight, arrived)
    copy.start()
    first = pl.multiple_of(place[1] * 32, 32)
    for c in range(2):
        for t in range(9):
            width = 128 if t < 8 else SH
            mask[c, t, :, :width] = here[c, :, t * 128 : t * 128 + width].astype(F32)
        for t in range(8):
            share[c, t] = pupil[c, pl.ds(first, 32), t * 128 : (t + 1) * 128]
    copy.wait()
    upper = lax.broadcasted_iota(jnp.int32, (8, NC), 0) >= 4
    wanted = upper == (place[1] == 1)
    four[...] = jnp.where(wanted, eight[...], pltpu.roll(eight[...], 4, 0))


def rows_kernel(
    gathered, table, here, beyond, share, far, out, windows, roots, near, scal, mask, fields, arrived, loaded
):
    copy = pltpu.make_async_copy(gathered, scal, arrived)
    copy.start()
    load = pltpu.make_async_copy(far, near, loaded)
    load.start()
    for c in range(2):
        for t in range(9):
            width = 128 if t < 8 else SH
            mask[c, t, 0:64, :width] = here[c, t, :, :width]
            mask[c, t, 64:128, :width] = beyond[c, :, t * 128 : t * 128 + width].astype(F32)
    copy.wait()
    for m in range(2):
        for p in range(16):
            at = m * 64 + p * 4
            roots[at : at + 4, :] = jnp.full((4, 128), scal[p, 0, 3 * m + 2])
    lane = lax.broadcasted_iota(jnp.int32, (32, 128), 1)
    sign = -lane_sign((128, 128))

    def build(p, field, at):
        first = [scal[p, 0, 3 * m + 1].astype(jnp.int32) for m in range(2)]
        by = [scal[p, 0, 3 * m].astype(jnp.int32) for m in range(2)]
        turn = [(128 - a) & 127 for a in by]
        keep = [lane < 128 - a for a in by]

        def turned(c, t, m):
            return pltpu.roll(mask[c, t, pl.ds(first[m], 32), :].astype(BF16), turn[m], 1)

        before = [[turned(c, 0, m) for c in range(2)] for m in range(2)]
        for t in range(8):
            cols = slice(t * 128, (t + 1) * 128)
            pr, pi = share[0, t], share[1, t]
            for m in range(2):
                after = [turned(c, t + 1, m) for c in range(2)]
                parts = [jnp.where(keep[m], before[m][c], after[c]) for c in range(2)]
                wr, wi = [part.astype(F32) for part in parts]
                before[m] = after
                low, high = m * 32, 64 + m * 32
                field[at + low : at + low + 32, cols] = (pr * wr - pi * wi).astype(BF16)
                field[at + high : at + high + 32, cols] = (pr * wi + pi * wr).astype(BF16)
                windows[p, low : low + 32, cols] = parts[0]
                windows[p, high : high + 32, cols] = parts[1]

    def transform(g, field):
        mixed = []
        for half in range(2):
            rows = field[half * 256 : (half + 1) * 256, :]
            both = lax.dot_general(table[...], rows, NT, preferred_element_type=F32)
            for n in range(2):
                p = 4 * g + 2 * half + n
                by_cos = both[:128, n * 128 : (n + 1) * 128]
                by_sin = both[128:, n * 128 : (n + 1) * 128]
                root = root_columns(scal[p, 0, 2], scal[p, 0, 5]) * (1.0 / K)
                mixed.append(((by_cos + sign * pltpu.roll(by_sin, 64, 1)) * root).reshape(16, 8, 128))
        first, second = swap_rows(mixed[0], mixed[1]), swap_rows(mixed[2], mixed[3])
        for n in range(2):
            tile = jnp.concatenate([first[n], second[n]], axis=1).astype(BF16)
            out[:, n, g * 16 : (g + 1) * 16, :] = tile

    for g in range(5):
        if g < 4:
            for n in range(4):
                build(4 * g + n, fields.at[g], n * 128)
        if g > 0:
            transform(g - 1, fields.at[g - 1])
    load.wait()


def swap_halves(a, b):
    low = (lax.broadcasted_iota(jnp.int32, a.shape, 1) & 32) == 0
    return jnp.where(low, a, pltpu.roll(b, 32, 1)), jnp.where(low, pltpu.roll(a, 96, 1), b)


def image_kernel(x, order, table, measured, roots, y, intensity, left, back, parts):
    sign = lane_sign((128, 128))
    stacked = []
    for q in range(4):
        tiles = []
        for rr in range(4):
            r = 4 * q + rr
            tiles.append(jnp.concatenate(swap_halves(x[2 * r], x[2 * r + 1]), axis=0))
        stacked.append(jnp.concatenate(tiles, axis=1))
    sorted_lanes = jnp.dot(jnp.concatenate(stacked, axis=0), order[...], preferred_element_type=F32)
    for q in range(4):
        for f0 in range(4):
            tile = sorted_lanes[q * 128 : (q + 1) * 128, f0 * 128 : (f0 + 1) * 128]
            left[f0, 0:128, q * 128 : (q + 1) * 128] = (tile * sign).astype(BF16)
            left[f0, 128:256, q * 128 : (q + 1) * 128] = pltpu.roll(tile.astype(BF16), 64, 1)

    upper = lax.broadcasted_iota(jnp.int32, (8, 128), 0) < 4
    for n in range(4):
        cols = slice(n * 256, (n + 1) * 256)
        h = [jnp.dot(left[f0], table[f0, :, cols], preferred_element_type=F32) for f0 in range(4)]
        s02, d02, s13, d13 = h[0] + h[2], h[0] - h[2], h[1] + h[3], h[1] - h[3]
        turned = jnp.concatenate([-d13[128:], d13[:128]], axis=0)
        fields = [s02 + s13, d02 + turned, s02 - s13, d02 - turned]
        scaled = []
        for y1 in range(4):
            e = fields[y1].reshape(2, 16, 8, 256)
            power = jnp.sum(e[0] * e[0] + e[1] * e[1], axis=0)
            power = (power + pltpu.roll(power, 4, 0)) * (1.0 / SOURCES)
            intensity[y1 * 4 + n] = jnp.where(upper, power[:, :128], power[:, 128:])
            residual = power - measured[:, y1 * 1024 + n * 256 : y1 * 1024 + (n + 1) * 256]
            scaled.append((e * (residual * GRAD_SCALE)[None, None]).reshape(256, 256))
        s02, d02 = scaled[0] + scaled[2], scaled[0] - scaled[2]
        s13, d13 = scaled[1] + scaled[3], scaled[1] - scaled[3]
        turned = jnp.concatenate([-d13[128:], d13[:128]], axis=0)
        back[0, :, cols] = (s02 + s13).astype(BF16)
        back[1, :, cols] = (d02 - turned).astype(BF16)
        back[2, :, cols] = (s02 - s13).astype(BF16)
        back[3, :, cols] = (d02 + turned).astype(BF16)

    for f0 in range(4):
        both = lax.dot_general(back[f0], table[f0], NT, preferred_element_type=F32)
        for q in range(4):
            cols = slice(q * 128, (q + 1) * 128)
            mixed = sign * both[:128, cols] + pltpu.roll(both[128:, cols], 64, 1)
            parts[q, :, f0 * 128 : (f0 + 1) * 128] = (mixed * roots[...]).astype(BF16)
    lined = lax.dot_general(parts[...].reshape(512, 512), order[...], NT, preferred_element_type=F32)
    for q in range(4):
        for rr in range(4):
            tile = lined[q * 128 : (q + 1) * 128, rr * 128 : (rr + 1) * 128].astype(BF16)
            y[8 * q + 2 * rr], y[8 * q + 2 * rr + 1] = swap_halves(tile[:64], tile[64:])


def gradient_kernel(y, table, windows, intensity, out, total):
    sign = lane_sign((128, 128)).astype(BF16)
    lefts = []
    for g in range(4):
        tiles = [y[:, n, g * 16 : (g + 1) * 16, :].astype(F32) for n in range(2)]
        for half in range(2):
            part = slice(half * 8, (half + 1) * 8)
            for u in swap_rows(tiles[0][:, part], tiles[1][:, part]):
                u = u.reshape(128, 128).astype(BF16)
                lefts.append(jnp.concatenate([u, sign * pltpu.roll(u, 64, 1)], axis=0))
    for n in range(4):
        cols = slice(n * 256, (n + 1) * 256)
        real = imag = 0.0
        for g in range(4):
            left = jnp.concatenate(lefts[4 * g : 4 * g + 4], axis=1)
            v = lax.dot_general(left, table[:, cols], TN, preferred_element_type=F32)
            for m in range(4):
                vr, vi = v[m * 128 : m * 128 + 64], v[m * 128 + 64 : m * 128 + 128]
                w = windows[4 * g + m, :, cols].astype(F32)
                wr, wi = w[:64], w[64:]
                real = real + (wr * vr + wi * vi)
                imag = imag + (wr * vi - wi * vr)
        total[0:64, cols] = real
        total[64:128, cols] = imag

    for t in range(8):
        cols = slice(t * 128, (t + 1) * 128)
        real = total[0:32, cols] + total[32:64, cols]
        imag = total[64:96, cols] + total[96:128, cols]
        turned = jnp.concatenate([real, imag], axis=0).T
        for n in range(2):
            both = jnp.concatenate([turned[n * 64 : n * 64 + 32], turned[n * 64 + 32 : n * 64 + 64]], axis=1)
            out[8 * n + t, 0:4] = both.reshape(4, 8, 128).astype(BF16)
    for yl in range(2):
        for z in range(8):
            out[8 * yl + z, 4] = intensity[2 * z + yl].astype(BF16)


def final_kernel(parts, grad, image):
    for yl in range(2):
        total = jnp.sum(
            jnp.stack([parts[8 * yl + z, 0:4].astype(F32).reshape(32, 128) for z in range(NZ)]), axis=0
        )
        for h in range(2):
            for c in range(2):
                start = h * 64 + c * 32
                grad[c, h * 32 : (h + 1) * 32, yl * 32 : (yl + 1) * 32] = total[:, start : start + 32]
    for j in range(16):
        power = parts[j % 2 * 8 + j // 2, 4].astype(F32)
        for h in range(2):
            image[4 * j : 4 * j + 4, h * 128 : (h + 1) * 128] = power[4 * h : 4 * h + 4]


def vmem(count):
    return [pl.BlockSpec(memory_space=pltpu.VMEM)] * count


HBM = pl.BlockSpec(memory_space=pltpu.HBM)
ANY = pl.BlockSpec(memory_space=pl.ANY)
SMEM = pl.BlockSpec(memory_space=pltpu.SMEM)
SMALL = pltpu.CompilerParams(vmem_limit_bytes=6 * 1024 * 1024)
PARAMS = pltpu.CompilerParams(vmem_limit_bytes=VMEM_LIMIT)


def kept(array):
    return pltpu.with_memory_space_constraint(array, pltpu.VMEM)


def own_kernel(shifts, weights, out):
    place = lax.broadcasted_iota(jnp.int32, (16, 128), 1)
    column = ((lax.broadcasted_iota(jnp.int32, (16, 128), 0) & 1) * 32).astype(F32)
    own = column
    for m in range(2):
        own = jnp.where(place == 3 * m, shifts[m, 0].astype(F32), own)
        own = jnp.where(place == 3 * m + 1, shifts[m, 1].astype(F32) + column, own)
        own = jnp.where(place == 3 * m + 2, jnp.sqrt(jnp.full((16, 128), weights[m])), own)
    out[:, 0, :] = own


def own_call(shifts, weights):
    return pl.pallas_call(
        own_kernel,
        out_shape=pltpu.VMEM((16, 1, 128), F32),
        in_specs=[SMEM, SMEM],
        out_specs=vmem(1)[0],
        name="own",
    )(shifts, weights)


def stage_call(place, here, pupil, measured):
    return pl.pallas_call(
        stage_kernel,
        out_shape=(
            pltpu.VMEM((2, 9, 64, 128), F32),
            pltpu.VMEM((2, 8, 32, 128), F32),
            pltpu.VMEM((8, NC), F32),
        ),
        in_specs=[SMEM] + vmem(2) + [HBM],
        out_specs=tuple(vmem(3)),
        scratch_shapes=[pltpu.VMEM((8, NC), F32), pltpu.SemaphoreType.DMA],
        compiler_params=SMALL,
        name="stage",
    )(place, here, pupil, pltpu.with_memory_space_constraint(measured, pltpu.HBM))


def rows_call(scal, table, here, beyond, share):
    far = pltpu.with_memory_space_constraint(jnp.asarray(col_tables()), pltpu.HBM)
    return pl.pallas_call(
        rows_kernel,
        out_shape=(
            jax.ShapeDtypeStruct((16, 2, 64, 128), BF16),
            pltpu.VMEM((16, 128, K), BF16),
            pltpu.VMEM((128, 128), F32),
            pltpu.VMEM((4, 512, 1024), BF16),
        ),
        in_specs=[ANY] + vmem(4) + [HBM],
        out_specs=tuple(vmem(4)),
        scratch_shapes=[
            pltpu.SMEM((16, 1, 128), F32),
            pltpu.VMEM((2, 9, 128, 128), F32),
            pltpu.VMEM((4, 512, K), BF16),
            pltpu.SemaphoreType.DMA,
            pltpu.SemaphoreType.DMA,
        ],
        compiler_params=PARAMS,
        name="rows",
    )(scal, kept(table), kept(here), kept(beyond), kept(share), far)


def image_call(x, table, measured, roots):
    return pl.pallas_call(
        image_kernel,
        out_shape=(
            jax.ShapeDtypeStruct((DEST, 64, 128), BF16),
            pltpu.VMEM((16, 8, 128), F32),
        ),
        in_specs=vmem(5),
        out_specs=tuple(vmem(2)),
        scratch_shapes=[
            pltpu.VMEM((4, 256, 512), BF16),
            pltpu.VMEM((4, 256, 1024), BF16),
            pltpu.VMEM((4, 128, 512), BF16),
        ],
        compiler_params=PARAMS,
        name="image",
    )(x, kept(jnp.asarray(lane_order())), kept(table), kept(measured), kept(roots))


def gradient_call(y, table, windows, intensity):
    return pl.pallas_call(
        gradient_kernel,
        out_shape=jax.ShapeDtypeStruct((16, 5, 8, 128), BF16),
        in_specs=vmem(4),
        out_specs=vmem(1)[0],
        scratch_shapes=[pltpu.VMEM((128, K), F32)],
        compiler_params=PARAMS,
        name="gradient",
    )(y.reshape(16, 2, 64, 128), kept(table), kept(windows), kept(intensity))


def final_call(parts):
    return pl.pallas_call(
        final_kernel,
        out_shape=(jax.ShapeDtypeStruct((2, 64, 64), F32), jax.ShapeDtypeStruct((64, 256), F32)),
        in_specs=vmem(1),
        out_specs=tuple(vmem(2)),
        compiler_params=SMALL,
        name="final",
    )(kept(parts))


def exchange(blocks, axes):
    return lax.all_to_all(blocks, axes, split_axis=0, concat_axis=0, tiled=True)


def shards(pupil, mask_spectrum, shifts, weights, measured):
    z, yl = lax.axis_index("z"), lax.axis_index("yl")
    mask = mask_spectrum.transpose(0, 2, 1)
    scal = exchange(own_call(shifts, weights), ("z", "yl"))
    beyond = lax.ppermute(mask, "row", [(i + 1, i) for i in range(NROW - 1)])
    place = jnp.stack([z, yl]).astype(jnp.int32)
    here, share, four = stage_call(place, mask, pupil.transpose(0, 2, 1), measured)
    table = lax.dynamic_index_in_dim(jnp.asarray(row_tables()), z, 0, keepdims=False)
    blocks, windows, roots, near = rows_call(scal, table, here, beyond, share)
    blocks, intensity = image_call(exchange(blocks.reshape(DEST, 64, 128), ("row", "yl")), near, four, roots)
    blocks = exchange(blocks, ("row", "yl"))
    parts = exchange(gradient_call(blocks, table, windows, intensity), ("yl", "z"))
    return final_call(parts)


def solution(mesh):
    finer = Mesh(mesh.devices.reshape(NZ, NYL, NROW), ("z", "yl", "row"))
    src = ("z", "yl")
    return jax.shard_map(
        shards,
        mesh=finer,
        in_specs=(
            P(None, None, "row"),
            P(None, None, "row"),
            P(src, None),
            P(src),
            P("row", None),
        ),
        out_specs=(P(None, src, "row"), P("row", src)),
        check_vma=False,
    )
```
